512 devices in a mesh: dp: 32 (over x, y), tensor: 16 (over z, core).
Axes of the slice: x: 4, y: 8, z: 8, core: 2. Of those that a mesh axis runs over, the one named last changes fastest.
Arguments:
- tokens: bfloat16 [4096, 8192], P('dp', 'tensor'), may hold values from -6 to 6
- base_weight: bfloat16 [8192, 8192], P('tensor', 'dp'), may hold values from -4 to 4
- adapter_down: bfloat16 [32, 16, 8192], P(None, None, 'tensor'), may hold values from -0.0625 to 0.0625
- adapter_up: bfloat16 [32, 16, 8192], P(None, None, 'dp'), may hold values from -1.5 to 1.5
- magnitude: float32 [32, 8192], P(None, 'tensor'), may hold values from 0.5 to 2
- tenant: int32 [16], replicated, may hold values from 0 to 31
- cotangent: bfloat16 [4096, 8192], P('dp', 'tensor'), may hold values from -0.29882812 to 0.29882812
Outputs:
- projected: bfloat16 [4096, 8192], P('dp', 'tensor')
- grad_down: float32 [32, 16, 8192], P(None, None, 'tensor')
- grad_up: float32 [32, 16, 8192], P(None, None, 'tensor')
- grad_magnitude: float32 [32, 8192], P(None, 'tensor')
The draws below stay inside these ranges and needn't reach their ends.
All inputs are finite; a program needn't handle non-finite values.
Results may differ from the reference program's by a relative error of at most 0.001.
Values may be sent and summed in bfloat16 or wider, within the bound.
A program may use at most 64 MiB of HBM per device.

```python
import math
import jax
import jax.numpy as jnp
import numpy as np
from jax import lax

D = 8192
TEN = 32
R = 16
STRETCH = 256
TOKENS = 4096
STRETCHES = 16
N_TENSOR = 16


def draw_base_weight(key, part):
    key = jax.random.fold_in(key, 11)
    key_values, key_rows, key_cols = jax.random.split(key, 3)
    values = jnp.clip(jax.random.normal(key_values, (D, D), jnp.float32), -4.0, 4.0)
    rising = 3.0
    factor = 1.0 / (4.5 * math.sqrt(D))
    position = jnp.arange(D, dtype=jnp.float32) / D
    row_scale = jnp.exp(math.log(rising) * position) * jnp.exp(math.log(4.0) * jax.random.uniform(key_rows, (D,), jnp.float32))
    col_scale = jnp.exp(math.log(10.0) * jax.random.uniform(key_cols, (D,), jnp.float32))
    result = jnp.clip(values * row_scale[:, None] * col_scale[None, :] * factor, -4.0, 4.0)
    return result.astype(jnp.bfloat16)


def plant(values, rng, smallest, largest):
    longest = values.shape.index(max(values.shape))
    spots = []
    for shift in (0, 1):
        where = [jax.random.randint(jax.random.fold_in(rng, axis), (), 0, length) for axis, length in enumerate(values.shape)]
        where[longest] = (where[longest] + shift) % values.shape[longest]
        spots.append(tuple(where))
    return values.at[spots[0]].set(smallest).at[spots[1]].set(largest)


def block_levels(stream_key, shape, cuts, smallest, top_value):
    gain = 1.0
    for dim, shards_of in cuts:
        draws = jax.random.uniform(jax.random.fold_in(jax.random.fold_in(stream_key, 6), dim), (shards_of,), jnp.float32, smallest / len(cuts), top_value / len(cuts))
        gain = gain * jnp.repeat(jnp.exp(draws), shape[dim] // shards_of).reshape((-1,) + (1,) * (len(shape) - 1 - dim))
    return gain


def cumulative_ranks(count, skew):
    portions = [(1 << 20) // math.isqrt(rank ** skew) + 1 for rank in range(1, count + 1)]
    deviation = 1 + sum(portions) // (1 << 30)
    return np.cumsum(np.array([max(1, weight // deviation) for weight in portions]))


def ranked(stream_key, extent, number_of, slope):
    listing = cumulative_ranks(number_of, slope)
    ticket = jax.random.randint(jax.random.fold_in(stream_key, 1), extent, 0, int(listing[number_of - 1]))
    standing = jnp.searchsorted(jnp.asarray(listing, jnp.int32), ticket, side="right")
    return jax.random.permutation(jax.random.fold_in(stream_key, 2), number_of)[standing].astype(jnp.int32)


def scatter_about(own_key, extent, width, limit, shards=(), kind=jnp.bfloat16):
    values = width * jax.random.normal(own_key, extent, jnp.float32)
    if shards:
        values = values * block_levels(own_key, extent, shards, -0.22, 0.18)
    return jnp.clip(values, -limit, limit).astype(kind)


def setup_inputs(seed: int = 0) -> dict:
    key_of = jax.random.split(jax.random.key(seed), 8)
    tokens = scatter_about(key_of[0], (TOKENS, D), 1.0, 6.0, ((0, 32), (1, 16)))
    base_weight = draw_base_weight(jax.random.fold_in(key_of[7], 71), 0)
    adapter_down = scatter_about(key_of[2], (TEN, R, D), D ** -0.5, 0.0625, ((2, 16),))
    adapter_up = scatter_about(key_of[3], (TEN, R, D), 0.25, 1.5, ((2, 32),))
    magnitude = jnp.clip(jnp.exp(math.log(2.0) - 1.3862944 * jax.random.uniform(key_of[4], (TEN, D), jnp.float32) ** block_levels(key_of[4], (TEN, D), ((1, 16),), -0.2, 0.2)), 0.5, 2.0)
    tenant = plant(ranked(key_of[5], (STRETCHES,), TEN, 2), jax.random.fold_in(key_of[5], 3), 0, TEN - 1).astype(jnp.int32)
    cotangent = scatter_about(key_of[6], (TOKENS, D), 0.05, 0.29882812, ((0, 32), (1, 16)))
    return dict(tokens=tokens, base_weight=base_weight, adapter_down=adapter_down, adapter_up=adapter_up, magnitude=magnitude, tenant=tenant, cotangent=cotangent)


def column_squares(base_f32, operands):
    down_rows, up_rows = operands
    combined = base_f32 + jnp.dot(down_rows.T, up_rows, precision=lax.Precision.HIGHEST)
    return lax.optimization_barrier(jnp.sum(combined * combined, axis=0))

def reference(tokens, base_weight, adapter_down, adapter_up, magnitude, tenant, cotangent):
    group_width = D // N_TENSOR
    chosen_down = adapter_down[tenant].astype(jnp.float32)
    chosen_up = adapter_up[tenant].astype(jnp.float32)
    blocks = tokens.reshape(STRETCHES, STRETCH, D)
    summed = jnp.zeros((STRETCHES, STRETCH, D), jnp.float32)
    rank_acts = jnp.zeros((STRETCHES, STRETCH, R), jnp.float32)
    for group_index in range(N_TENSOR):
        offset = group_index * group_width
        features = blocks[:, :, offset:offset + group_width]
        base_part = jnp.dot(features.reshape(-1, group_width), base_weight[offset:offset + group_width], preferred_element_type=jnp.float32).reshape(STRETCHES, STRETCH, D)
        rank_part = jnp.einsum('cik,crk->cir', features.astype(jnp.float32), chosen_down[:, :, offset:offset + group_width], precision=lax.Precision.HIGHEST)
        summed = summed + base_part
        rank_acts = rank_acts + rank_part
    summed = summed + jnp.einsum('cir,crn->cin', rank_acts, chosen_up, precision=lax.Precision.HIGHEST)
    base_f32 = base_weight.astype(jnp.float32)
    squares = lax.map(lambda operands: column_squares(base_f32, operands), (chosen_down, chosen_up))
    column_norm = jnp.sqrt(squares + 1e-06)
    scaling = magnitude[tenant] / column_norm
    projected = (summed * scaling[:, None, :]).reshape(TOKENS, D).astype(jnp.bfloat16)
    cotan = cotangent.reshape(STRETCHES, STRETCH, D).astype(jnp.float32)
    scaled = cotan * scaling[:, None, :]
    up_terms = jnp.einsum('cir,cin->crn', rank_acts, scaled, precision=lax.Precision.HIGHEST)
    rank_back = jnp.einsum('cin,crn->cir', scaled, chosen_up, precision=lax.Precision.HIGHEST)
    down_terms = jnp.einsum('cir,cik->crk', rank_back, blocks.astype(jnp.float32), precision=lax.Precision.HIGHEST)
    mag_terms = lax.optimization_barrier(jnp.sum(cotan * summed / column_norm[:, None, :], axis=1))
    onehot = (tenant[:, None] == jnp.arange(TEN, dtype=jnp.int32)[None, :]).astype(jnp.float32)
    grad_down = jnp.einsum('ct,crk->trk', onehot, down_terms, precision=lax.Precision.HIGHEST)
    grad_up = jnp.einsum('ct,crn->trn', onehot, up_terms, precision=lax.Precision.HIGHEST)
    grad_magnitude = jnp.einsum('ct,cn->tn', onehot, mag_terms, precision=lax.Precision.HIGHEST)
    return (projected, grad_down, grad_up, grad_magnitude)
```

```python
import functools

import jax
import jax.numpy as jnp
from jax import lax
from jax.experimental import pallas as pl
from jax.experimental.pallas import tpu as pltpu
from jax.sharding import PartitionSpec as P

X_CHIPS = 4
RANK = 16
F32 = jnp.float32
BF16 = jnp.bfloat16


def send_to(src, dst, send_sem, recv_sem, device):
    return pltpu.make_async_remote_copy(
        src_ref=src,
        dst_ref=dst,
        send_sem=send_sem,
        recv_sem=recv_sem,
        device_id=device,
        device_id_type=pl.DeviceIdType.MESH,
    )


def split3(value):
    high = value.astype(BF16)
    rest = value - high.astype(F32)
    middle = rest.astype(BF16)
    low = (rest - middle.astype(F32)).astype(BF16)
    return high, middle, low


def dot_nn(a, b):
    return jnp.dot(a, b, preferred_element_type=F32)


def dot_nt(a, b):
    return lax.dot_general(a, b, (((1,), (1,)), ((), ())), preferred_element_type=F32)


def dot_tn(a, b):
    return lax.dot_general(a, b, (((0,), (0,)), ((), ())), preferred_element_type=F32)


def halves_of(flow, step, count):
    if step < count // 2 - 1:
        return (0, 1)
    return (flow,)


def exchange_kernel(
    nx, ny, nt,
    tenant, tok, w, down, up, mag, cot,
    proj_out, g_out, m_out,
    tok_g, w_g, up_sel, up_g, down_sel, cot_l, mag_s, mag_l,
    ex_s, ex_l, rank_p, parts, sib, ring,
    scaled_s, f_s, f_l, h_s, h_l, rank_s, u_s, g, proj_s, proj_l, m_s, m_g,
    tok_ss, tok_rs, w_ss, w_rs, up_ss, up_rs, cot_ss, cot_rs, mag_ss, mag_rs,
    ex_ss, ex_rs, sib_ss, sib_rs, ring_ss, ring_rs, f_ss, f_rs, h_ss, h_rs,
    u_ss, u_rs, gy_ss, gy_rs, gx_ss, gx_rs, pr_ss, pr_rs, m_ss, m_rs,
    my_ss, my_rs, mx_ss, mx_rs,
):
    s_per = ny // 2
    nz = nt // 2
    rpy = RANK // ny
    tb, kb = tok.shape
    cb = w.shape[1]
    dp = lax.axis_index("dp")
    t = lax.axis_index("tensor")
    x, y = lax.div(dp, ny), lax.rem(dp, ny)
    z, core = lax.div(t, 2), lax.rem(t, 2)
    xq, cl = lax.div(t, s_per), lax.rem(t, s_per)
    y_half, y_par = lax.div(y, 2), lax.rem(y, 2)
    at_home = y_half == cl

    def dev(x2, y2, t2):
        return (x2 * ny + y2, t2)

    def wrap(value, count):
        return lax.rem(value + 2 * count, count)

    def on_y(i):
        return dev(x, wrap(y + i, ny), t)

    def on_x(i):
        return dev(wrap(x + i, nx), y, t)

    def on_t(i):
        return dev(x, y, wrap(t + i, nt))

    def on_z(i):
        return dev(x, y, 2 * wrap(z + i, nz) + core)

    sibling = dev(x, y, 2 * z + 1 - core)
    swap = [dev(x, 2 * cl + p, s_per * xq + y_half) for p in (0, 1)]
    swap_own = dev(x, 2 * cl + y_par, s_per * xq + y_half)

    barrier = pltpu.get_barrier_semaphore()

    def greet(device):
        pl.semaphore_signal(barrier, inc=1, device_id=device, device_id_type=pl.DeviceIdType.MESH)

    @pl.loop(1, ny)
    def _(i):
        greet(on_y(i))

    @pl.loop(1, nx)
    def _(i):
        greet(on_x(i))

    @pl.loop(1, nt)
    def _(i):
        greet(on_t(i))

    for p in (0, 1):
        @pl.when(jnp.logical_not(jnp.logical_and(at_home, y_par == p)))
        def _():
            greet(swap[p])

    tok_g[y] = tok[...].reshape(2, tb // 2, kb)
    w_g[x] = w[...].reshape(2, kb // 2, cb)
    for c in range(nx * s_per):
        up_sel[c // s_per, c % s_per] = up[tenant[c]]
    up_g[x] = up_sel[x]
    for c in range(s_per):
        down_sel[pl.ds(c * RANK, RANK), :] = down[tenant[x * s_per + c]]
    row_ids = lax.broadcasted_iota(jnp.int32, mag.shape, 0)
    mag_row = jnp.sum(jnp.where(row_ids == tenant[x * s_per + y_half], mag[...], 0.0), axis=0, keepdims=True)
    for p in (0, 1):
        mag_s[p] = jnp.broadcast_to(mag_row[:, p * cb:(p + 1) * cb], (8, cb))
    ex_s[...] = jnp.zeros_like(ex_s)
    f_s[...] = jnp.zeros_like(f_s)
    m_s[...] = jnp.zeros_like(m_s)

    others = (ny - 1) + (nx - 1) + (nt - 1)

    @pl.when(at_home)
    def _():
        pl.semaphore_wait(barrier, others + 1)

    @pl.when(jnp.logical_not(at_home))
    def _():
        pl.semaphore_wait(barrier, others + 2)

    def tok_copy(flow, step, h):
        sign = 1 if flow == 0 else -1
        block = wrap(y - sign * step, ny)
        slot = tok_g.at[block, h]
        return send_to(slot, slot, tok_ss.at[flow, step, h], tok_rs.at[flow, step, h], on_y(sign))

    def tok_arrival(flow, step, h):
        sign = 1 if flow == 0 else -1
        slot = tok_g.at[wrap(y - sign * (step + 1), ny), h]
        return send_to(slot, slot, tok_ss.at[flow, step, h], tok_rs.at[flow, step, h], on_y(sign))

    def w_copy(flow, step, h):
        sign = 1 if flow == 0 else -1
        slot = w_g.at[wrap(x - sign * step, nx), h]
        return send_to(slot, slot, w_ss.at[flow, step, h], w_rs.at[flow, step, h], on_x(sign))

    def w_arrival(flow, step, h):
        sign = 1 if flow == 0 else -1
        slot = w_g.at[wrap(x - sign * (step + 1), nx), h]
        return send_to(slot, slot, w_ss.at[flow, step, h], w_rs.at[flow, step, h], on_x(sign))

    for h in (0, 1):
        for flow in (0, 1):
            if h in halves_of(flow, 0, ny):
                tok_copy(flow, 0, h).start()
            if h in halves_of(flow, 0, nx):
                w_copy(flow, 0, h).start()

    def up_copy(i):
        return send_to(up_sel.at[wrap(x + i, nx)], up_g.at[x], up_ss.at[i], up_rs.at[i], on_x(i))

    def up_arrival(i):
        slot = up_g.at[wrap(x - i, nx)]
        return send_to(slot, slot, up_ss.at[i], up_rs.at[i], on_x(i))

    for i in range(1, nx):
        up_copy(i).start()

    def cot_copy(p):
        return send_to(cot.at[:, pl.ds(p * cb, cb)], cot_l.at[y_par], cot_ss.at[p], cot_rs.at[y_par], swap[p])

    def cot_arrival(p):
        return send_to(cot_l.at[p], cot_l.at[p], cot_ss.at[p], cot_rs.at[p], swap[p])

    def mag_copy(p):
        return send_to(mag_s.at[p], mag_l.at[y_par], mag_ss.at[p], mag_rs.at[y_par], swap[p])

    def mag_arrival(p):
        return send_to(mag_l.at[p], mag_l.at[p], mag_ss.at[p], mag_rs.at[p], swap[p])

    stays = [jnp.logical_and(at_home, y_par == p) for p in (0, 1)]
    for p in (0, 1):
        @pl.when(jnp.logical_not(stays[p]))
        def _():
            cot_copy(p).start()
            mag_copy(p).start()

        @pl.when(stays[p])
        def _():
            cot_l[p] = cot[:, p * cb:(p + 1) * cb]
            mag_l[p] = mag_s[p]

    for step in range(ny // 2):
        for h in (0, 1):
            for flow in (0, 1):
                if h in halves_of(flow, step, ny):
                    tok_arrival(flow, step, h).wait_recv()
                    if step + 1 < ny // 2 and h in halves_of(flow, step + 1, ny):
                        tok_copy(flow, step + 1, h).start()
                if step < nx // 2 and h in halves_of(flow, step, nx):
                    w_arrival(flow, step, h).wait_recv()
                    if step + 1 < nx // 2 and h in halves_of(flow, step + 1, nx):
                        w_copy(flow, step + 1, h).start()
    for i in range(1, nx):
        up_arrival(i).wait_recv()

    def stretch_tokens(c):
        return tok_g[pl.ds(2 * c, 2)].reshape(2 * tb, kb)

    for c in range(s_per):
        rank_p[c] = dot_nt(down_sel[pl.ds(c * RANK, RANK), :], stretch_tokens(c))
    grams = []
    for c in range(s_per):
        rows = down_sel[pl.ds(c * RANK, RANK), :]
        grams.append(jnp.concatenate(split3(dot_nt(rows, rows)), axis=0))

    @pl.loop(0, nx)
    def _(xb):
        block = w_g[xb].reshape(kb, cb)
        block_f32 = block.astype(F32)
        base = jnp.sum(block_f32 * block_f32, axis=0, keepdims=True)
        crossed = dot_nn(down_sel[...], block)
        for c in range(s_per):
            rows = up_g[xb, c]
            quad = dot_tn(grams[c], jnp.concatenate([rows, rows, rows], axis=0))
            mixed = rows.astype(F32) * (2.0 * crossed[c * RANK:(c + 1) * RANK] + quad)
            squares = base + jnp.sum(mixed, axis=0, keepdims=True)
            own = rank_p[c]
            picked = own[0:rpy]
            for y2 in range(1, ny):
                picked = jnp.where(y == y2, own[y2 * rpy:(y2 + 1) * rpy], picked)
            slot = xb * s_per + c
            ex_s[slot, 0:1, :] = squares[:, :cb // 2]
            ex_s[slot, 1:2, :] = squares[:, cb // 2:]
            ex_s[slot, 2:2 + rpy, :] = picked[:, :tb]
            ex_s[slot, 2 + rpy:2 + 2 * rpy, :] = picked[:, tb:]

    def ex_copy(i):
        return send_to(ex_s.at[wrap(t + i, nt)], ex_l.at[t], ex_ss.at[i], ex_rs.at[i], on_t(i))

    def ex_arrival(i):
        slot = ex_l.at[wrap(t - i, nt)]
        return send_to(slot, slot, ex_ss.at[i], ex_rs.at[i], on_t(i))

    @pl.loop(1, nt)
    def _(i):
        ex_copy(i).start()

    ex_l[t] = ex_s[t]

    half = nz // 2

    def place(i):
        return wrap(z + half + (1 - 2 * lax.rem(i, 2)) * lax.div(i + 1, 2), nz)

    def product(slot):
        xb, c = lax.div(slot, s_per), lax.rem(slot, s_per)
        result = dot_nn(stretch_tokens(c), w_g[xb].reshape(kb, cb))
        for p in (0, 1):
            for j in (0, 1):
                parts[slot, 2 * p + j] = result[p * tb:(p + 1) * tb, j * (cb // 2):(j + 1) * (cb // 2)]

    def sib_copy(i):
        zb = place(i)
        return send_to(parts.at[2 * zb + 1 - core], sib.at[zb], sib_ss.at[i], sib_rs.at[i], sibling)

    def sib_arrival(i):
        slot = sib.at[place(i)]
        return send_to(slot, slot, sib_ss.at[i], sib_rs.at[i], sibling)

    @pl.loop(0, nz)
    def _(i):
        product(2 * place(i) + 1 - core)
        sib_copy(i).start()
        product(2 * place(i) + core)

    def ring_copy(flow, step, q):
        sign = 1 if flow == 0 else -1
        zb = wrap(z + sign * (half - step), nz)
        return send_to(
            parts.at[2 * zb + core, q], ring.at[flow, step, q],
            ring_ss.at[flow, step, q], ring_rs.at[flow, step, q], on_z(sign),
        )

    def ring_has(flow, step, q):
        return step > 0 or q // 2 == flow

    def ring_step(step, q):
        for flow in (0, 1):
            sign = 1 if flow == 0 else -1
            if not ring_has(flow, step, q):
                continue
            zb = wrap(z + sign * (half - step), nz)
            value = parts[2 * zb + core, q] + sib[zb, q]
            if step > 0 and ring_has(flow, step - 1, q):
                ring_copy(flow, step - 1, q).wait_recv()
                value = value + ring[flow, step - 1, q]
            parts[2 * zb + core, q] = value
            ring_copy(flow, step, q).start()

    def after_extras():
        @pl.loop(1, nt)
        def _(i):
            ex_arrival(i).wait_recv()

        for p in (0, 1):
            @pl.when(jnp.logical_not(stays[p]))
            def _():
                cot_arrival(p).wait_recv()
                mag_arrival(p).wait_recv()

        total = jnp.sum(ex_l[...], axis=0)
        squares = jnp.concatenate([total[0:1], total[1:2]], axis=1)
        norm = jnp.sqrt(squares + 1e-06)
        scaling = mag_l[0][0:1] / norm
        scaled = cot_l[...].reshape(2 * tb, cb).astype(F32) * scaling
        scaled_s[...] = scaled
        rows = up_g[xq, cl]
        pieces = split3(scaled)
        back = dot_nt(rows, pieces[0]) + (dot_nt(rows, pieces[1]) + dot_nt(rows, pieces[2]))
        for y2 in range(ny):
            f_s[y2, 0:2 * rpy, :] = total[2:2 + 2 * rpy]
            f_s[y2, 8:8 + rpy, :] = back[y2 * rpy:(y2 + 1) * rpy, :tb]
            f_s[y2, 8 + rpy:8 + 2 * rpy, :] = back[y2 * rpy:(y2 + 1) * rpy, tb:]

        @pl.loop(1, ny)
        def _(i):
            f_copy(i).start()

        f_l[y] = f_s[y]
        return norm, scaling

    def f_copy(i):
        return send_to(f_s.at[wrap(y + i, ny)], f_l.at[y], f_ss.at[i], f_rs.at[i], on_y(i))

    def f_arrival(i):
        slot = f_l.at[wrap(y - i, ny)]
        return send_to(slot, slot, f_ss.at[i], f_rs.at[i], on_y(i))

    def h_copy(i):
        return send_to(h_s, h_l.at[t], h_ss.at[i], h_rs.at[i], on_t(i))

    def h_arrival(i):
        slot = h_l.at[wrap(t - i, nt)]
        return send_to(slot, slot, h_ss.at[i], h_rs.at[i], on_t(i))

    def u_copy(p):
        return send_to(u_s.at[p], g.at[x, 2 * cl + p, y_par], u_ss.at[p], u_rs.at[y_par], swap[p])

    def u_arrival(p):
        slot = g.at[x, y, p]
        return send_to(slot, slot, u_ss.at[p], u_rs.at[p], swap[p])

    def after_f():
        @pl.loop(1, ny)
        def _(i):
            f_arrival(i).wait_recv()

        h_s[...] = jnp.sum(f_l[:, 8:16, :], axis=0)

        @pl.loop(1, nt)
        def _(i):
            h_copy(i).start()

        h_l[t] = h_s[...]
        for y2 in range(ny):
            rank_s[y2 * rpy:(y2 + 1) * rpy, :tb] = f_l[y2, 0:rpy, :]
            rank_s[y2 * rpy:(y2 + 1) * rpy, tb:] = f_l[y2, rpy:2 * rpy, :]
        a1, a2, a3 = split3(rank_s[...])
        b1, b2, b3 = split3(scaled_s[...])
        low = dot_nn(a3, b1) + dot_nn(a2, b2) + dot_nn(a1, b3)
        terms = dot_nn(a1, b1) + (dot_nn(a2, b1) + dot_nn(a1, b2) + low)
        for p in (0, 1):
            u_s[p, 0:8, :] = terms[8 * p:8 * p + 8, :cb // 2]
            u_s[p, 8:16, :] = terms[8 * p:8 * p + 8, cb // 2:]

            @pl.when(jnp.logical_not(stays[p]))
            def _():
                u_copy(p).start()

            @pl.when(stays[p])
            def _():
                g[x, y, p] = u_s[p]

    def gy_copy(i):
        slot = g.at[x, y]
        return send_to(slot, slot, gy_ss.at[i], gy_rs.at[i], on_y(i))

    def gy_arrival(i):
        slot = g.at[x, wrap(y - i, ny)]
        return send_to(slot, slot, gy_ss.at[i], gy_rs.at[i], on_y(i))

    def after_h():
        @pl.loop(1, nt)
        def _(i):
            h_arrival(i).wait_recv()

        for c in range(s_per):
            tile = h_l[c]
            for xb in range(1, nx):
                tile = tile + h_l[xb * s_per + c]
            stacked = jnp.concatenate([v.astype(F32) for v in split3(tile)] + [jnp.zeros_like(tile)], axis=0)
            stacked = stacked.astype(BF16)
            both = []
            for p in (0, 1):
                full = dot_nn(stacked, tok_g[2 * c + p].reshape(tb, kb))
                both.append(full[0:8] + (full[8:16] + full[16:24]))
            terms = both[0][0:rpy] + both[1][rpy:2 * rpy]
            for q in range(kb // 128):
                g[x, y, 2 + q // 2, 8 * (q % 2) + c * rpy:8 * (q % 2) + (c + 1) * rpy, :] = terms[:, 128 * q:128 * (q + 1)]
        for p in (0, 1):
            @pl.when(jnp.logical_not(stays[p]))
            def _():
                u_arrival(p).wait_recv()

        @pl.loop(1, ny)
        def _(i):
            gy_copy(i).start()

    def gx_copy(flow, step, h):
        sign = 1 if flow == 0 else -1
        slot = g.at[wrap(x - sign * step, nx), pl.ds(h * s_per, s_per)]
        return send_to(slot, slot, gx_ss.at[flow, step, h], gx_rs.at[flow, step, h], on_x(sign))

    def gx_arrival(flow, step, h):
        sign = 1 if flow == 0 else -1
        slot = g.at[wrap(x - sign * (step + 1), nx), pl.ds(h * s_per, s_per)]
        return send_to(slot, slot, gx_ss.at[flow, step, h], gx_rs.at[flow, step, h], on_x(sign))

    def after_gy():
        @pl.loop(1, ny)
        def _(i):
            gy_arrival(i).wait_recv()

        for flow in (0, 1):
            for h in halves_of(flow, 0, nx):
                gx_copy(flow, 0, h).start()

    def after_gx(step):
        for h in (0, 1):
            for flow in (0, 1):
                if h in halves_of(flow, step, nx):
                    gx_arrival(flow, step, h).wait_recv()
                    if step + 1 < nx // 2 and h in halves_of(flow, step + 1, nx):
                        gx_copy(flow, step + 1, h).start()

    sib_arrival(0).wait_recv()
    for q in range(4):
        ring_step(0, q)
    norm, scaling = after_extras()
    for step in range(1, half):
        sib_arrival(2 * step - 1).wait_recv()
        sib_arrival(2 * step).wait_recv()
        for q in range(4):
            ring_step(step, q)
            if step == 1 and q == 1:
                after_f()
            if step == 2 and q == 0:
                after_h()
            if step == 2 and q == 3:
                after_gy()
    if half < 3:
        if half < 2:
            after_f()
        after_h()
        after_gy()
    sib_arrival(nz - 1).wait_recv()

    rank_stack = jnp.concatenate(split3(rank_s[...]), axis=0)
    rows = up_g[xq, cl]
    low_rank = dot_tn(rank_stack, jnp.concatenate([rows, rows, rows], axis=0))
    mag_sum = [None, None]
    for q in range(4):
        p, j = q // 2, q % 2
        value = parts[t, q] + sib[z, q]
        for flow in (0, 1):
            if ring_has(flow, half - 1, q):
                ring_copy(flow, half - 1, q).wait_recv()
                value = value + ring[flow, half - 1, q]
        lanes = slice(j * (cb // 2), (j + 1) * (cb // 2))
        value = value + low_rank[p * tb:(p + 1) * tb, lanes]
        proj_s[p, :, lanes] = (value * scaling[:, lanes]).astype(BF16)
        term = jnp.sum(cot_l[p, :, lanes].astype(F32) * value, axis=0, keepdims=True)
        mag_sum[j] = term if mag_sum[j] is None else mag_sum[j] + term

    def pr_copy(p):
        return send_to(proj_s.at[p], proj_l.at[y_par], pr_ss.at[p], pr_rs.at[y_par], swap[p])

    def pr_arrival(p):
        return send_to(proj_l.at[p], proj_l.at[p], pr_ss.at[p], pr_rs.at[p], swap[p])

    for j in (0, 1):
        m_s[j:j + 1, :] = mag_sum[j] / norm[:, j * (cb // 2):(j + 1) * (cb // 2)]

    def m_copy():
        return send_to(m_s, m_g.at[x, 2 * cl + y_par], m_ss, m_rs, swap_own)

    def m_arrival():
        slot = m_g.at[x, y]
        return send_to(slot, slot, m_ss, m_rs, swap_own)

    @pl.when(jnp.logical_not(at_home))
    def _():
        m_copy().start()

    @pl.when(at_home)
    def _():
        m_g[x, y] = m_s[...]

    for p in (0, 1):
        @pl.when(jnp.logical_not(stays[p]))
        def _():
            pr_copy(p).start()

        @pl.when(stays[p])
        def _():
            proj_l[p] = proj_s[p]

    for step in range(nx // 2):
        after_gx(step)

    def my_copy(i):
        slot = m_g.at[x, y]
        return send_to(slot, slot, my_ss.at[i], my_rs.at[i], on_y(i))

    def my_arrival(i):
        slot = m_g.at[x, wrap(y - i, ny)]
        return send_to(slot, slot, my_ss.at[i], my_rs.at[i], on_y(i))

    def mx_copy(i):
        slot = m_g.at[x]
        return send_to(slot, slot, mx_ss.at[i], mx_rs.at[i], on_x(i))

    def mx_arrival(i):
        slot = m_g.at[wrap(x - i, nx)]
        return send_to(slot, slot, mx_ss.at[i], mx_rs.at[i], on_x(i))

    @pl.when(jnp.logical_not(at_home))
    def _():
        m_arrival().wait_recv()

    @pl.loop(1, ny)
    def _(i):
        my_copy(i).start()

    g_out[...] = g[...]
    for p in (0, 1):
        @pl.when(jnp.logical_not(stays[p]))
        def _():
            pr_arrival(p).wait_recv()

        proj_out[:, p * cb:(p + 1) * cb] = proj_l[p]

    @pl.loop(1, ny)
    def _(i):
        my_arrival(i).wait_recv()

    @pl.loop(1, nx)
    def _(i):
        mx_copy(i).start()

    for flow in (0, 1):
        for step in range(ny // 2):
            for h in halves_of(flow, step, ny):
                tok_copy(flow, step, h).wait_send()
        for step in range(nx // 2):
            for h in halves_of(flow, step, nx):
                w_copy(flow, step, h).wait_send()
                gx_copy(flow, step, h).wait_send()
        for step in range(half):
            for q in range(4):
                if ring_has(flow, step, q):
                    ring_copy(flow, step, q).wait_send()

    @pl.loop(1, nt)
    def _(i):
        ex_copy(i).wait_send()
        h_copy(i).wait_send()

    @pl.loop(0, nz)
    def _(i):
        sib_copy(i).wait_send()

    @pl.loop(1, ny)
    def _(i):
        f_copy(i).wait_send()
        gy_copy(i).wait_send()
        my_copy(i).wait_send()

    for p in (0, 1):
        @pl.when(jnp.logical_not(stays[p]))
        def _():
            cot_copy(p).wait_send()
            mag_copy(p).wait_send()
            u_copy(p).wait_send()
            pr_copy(p).wait_send()

    @pl.when(jnp.logical_not(at_home))
    def _():
        m_copy().wait_send()

    for i in range(1, nx):
        up_copy(i).wait_send()

    @pl.loop(1, nx)
    def _(i):
        mx_arrival(i).wait_recv()
        mx_copy(i).wait_send()

    m_out[...] = m_g[...]


def scatter_kernel(nx, ny, tenant, proj, g, m, proj_out, down_out, up_out, mag_out):
    s_per = ny // 2
    rpy = RANK // ny
    proj_out[...] = proj[...]
    down_out[...] = jnp.zeros_like(down_out)
    up_out[...] = jnp.zeros_like(up_out)
    row_ids = lax.broadcasted_iota(jnp.int32, (mag_out.shape[0], 128), 0)
    mag_sums = [jnp.zeros(row_ids.shape, F32)] * (mag_out.shape[1] // 128)
    quarters = up_out.shape[2] // 128
    for xb in range(nx):
        for c in range(s_per):
            who = tenant[xb * s_per + c]
            for p in (0, 1):
                for q in range(quarters):
                    up_out[who, 8 * p:8 * p + 8, 128 * q:128 * (q + 1)] += g[
                        xb, 2 * c + p, q // 2, 8 * (q % 2):8 * (q % 2) + 8, :
                    ]
            for q in range(quarters):
                rows = [
                    g[xb, yb, 2 + q // 2, 8 * (q % 2) + c * rpy:8 * (q % 2) + (c + 1) * rpy, :]
                    for yb in range(ny)
                ]
                down_out[who, :, 128 * q:128 * (q + 1)] += jnp.concatenate(rows, axis=0)
                row = m[xb, 2 * c + q // 2, q % 2:q % 2 + 1, :]
                mag_sums[q] = mag_sums[q] + jnp.where(row_ids == who, row, 0.0)
    for q in range(quarters):
        mag_out[:, 128 * q:128 * (q + 1)] = mag_sums[q]


def per_device(nx, ny, nt, tokens, base_weight, adapter_down, adapter_up, magnitude, tenant, cotangent):
    tb, kb = tokens.shape
    cb = base_weight.shape[1]
    tenants = adapter_down.shape[0]
    s_per = ny // 2
    nz = nt // 2
    rpy = RANK // ny
    ex_rows = -(-(2 + 2 * rpy) // 8) * 8
    dma = pltpu.SemaphoreType.DMA
    vmem = pl.BlockSpec(memory_space=pltpu.VMEM)
    smem = pl.BlockSpec(memory_space=pltpu.SMEM)
    scratch = [
        pltpu.VMEM((ny, 2, tb // 2, kb), BF16),
        pltpu.VMEM((nx, 2, kb // 2, cb), BF16),
        pltpu.VMEM((nx, s_per, RANK, cb), BF16),
        pltpu.VMEM((nx, s_per, RANK, cb), BF16),
        pltpu.VMEM((s_per * RANK, kb), BF16),
        pltpu.VMEM((2, tb, cb), BF16),
        pltpu.VMEM((2, 8, cb), F32),
        pltpu.VMEM((2, 8, cb), F32),
        pltpu.VMEM((nt, ex_rows, 128), F32),
        pltpu.VMEM((nt, ex_rows, 128), F32),
        pltpu.VMEM((s_per, RANK, 2 * tb), F32),
        pltpu.VMEM((nt, 4, tb, cb // 2), F32),
        pltpu.VMEM((nz, 4, tb, cb // 2), F32),
        pltpu.VMEM((2, nz // 2, 4, tb, cb // 2), F32),
        pltpu.VMEM((2 * tb, cb), F32),
        pltpu.VMEM((ny, 16, 128), F32),
        pltpu.VMEM((ny, 16, 128), F32),
        pltpu.VMEM((8, 128), F32),
        pltpu.VMEM((nt, 8, 128), F32),
        pltpu.VMEM((RANK, 2 * tb), F32),
        pltpu.VMEM((2, 16, 128), F32),
        pltpu.VMEM((nx, ny, 4, 16, 128), F32),
        pltpu.VMEM((2, tb, cb), BF16),
        pltpu.VMEM((2, tb, cb), BF16),
        pltpu.VMEM((8, 128), F32),
        pltpu.VMEM((nx, ny, 8, 128), F32),
    ]
    sems = [
        (2, ny // 2, 2), (2, nx // 2, 2), (nx,), (2,), (2,),
        (nt,), (nz,), (2, nz // 2, 4), (ny,), (nt,),
        (2,), (ny,), (2, nx // 2, 2), (2,), None,
        (ny,), (nx,),
    ]
    for shape in sems:
        scratch += [dma if shape is None else dma(shape)] * 2
    proj, gathered, mags = pl.pallas_call(
        functools.partial(exchange_kernel, nx, ny, nt),
        out_shape=(
            jax.ShapeDtypeStruct((tb, 2 * cb), BF16),
            jax.ShapeDtypeStruct((nx, ny, 4, 16, 128), F32),
            jax.ShapeDtypeStruct((nx, ny, 8, 128), F32),
        ),
        in_specs=[smem] + [vmem] * 6,
        out_specs=(vmem, vmem, vmem),
        scratch_shapes=scratch,
        compiler_params=pltpu.CompilerParams(
            collective_id=0, has_side_effects=True, vmem_limit_bytes=32 * 1024 * 1024
        ),
        name="exchange",
    )(tenant, tokens, base_weight, adapter_down, adapter_up, magnitude, cotangent)
    return pl.pallas_call(
        functools.partial(scatter_kernel, nx, ny),
        out_shape=(
            jax.ShapeDtypeStruct((tb, 2 * cb), BF16),
            jax.ShapeDtypeStruct((tenants, RANK, kb), F32),
            jax.ShapeDtypeStruct((tenants, RANK, 2 * cb), F32),
            jax.ShapeDtypeStruct((tenants, 2 * cb), F32),
        ),
        in_specs=[smem, vmem, vmem, vmem],
        out_specs=(vmem, vmem, vmem, vmem),
        compiler_params=pltpu.CompilerParams(vmem_limit_bytes=16 * 1024 * 1024),
        name="scatter",
    )(tenant, proj, gathered, mags)


def solution(mesh, nx=X_CHIPS):
    ny = mesh.shape["dp"] // nx
    nt = mesh.shape["tensor"]
    in_specs = (
        P("dp", "tensor"),
        P("tensor", "dp"),
        P(None, None, "tensor"),
        P(None, None, "dp"),
        P(None, "tensor"),
        P(),
        P("dp", "tensor"),
    )
    out_specs = (
        P("dp", "tensor"),
        P(None, None, "tensor"),
        P(None, None, "tensor"),
        P(None, "tensor"),
    )
    return jax.shard_map(
        functools.partial(per_device, nx, ny, nt),
        mesh=mesh, in_specs=in_specs, out_specs=out_specs, check_vma=False,
    )
```

```python
import functools

import jax
import jax.numpy as jnp
from jax import lax
from jax.experimental import pallas as pl
from jax.experimental.pallas import tpu as pltpu
from jax.sharding import PartitionSpec as P

X_CHIPS = 4
RANK = 16
F32 = jnp.float32
BF16 = jnp.bfloat16


def send_to(src, dst, send_sem, recv_sem, device):
    return pltpu.make_async_remote_copy(
        src_ref=src,
        dst_ref=dst,
        send_sem=send_sem,
        recv_sem=recv_sem,
        device_id=device,
        device_id_type=pl.DeviceIdType.MESH,
    )


def split3(value):
    high = value.astype(BF16)
    rest = value - high.astype(F32)
    middle = rest.astype(BF16)
    low = (rest - middle.astype(F32)).astype(BF16)
    return high, middle, low


def dot_nn(a, b):
    return jnp.dot(a, b, preferred_element_type=F32)


def dot_nt(a, b):
    return lax.dot_general(a, b, (((1,), (1,)), ((), ())), preferred_element_type=F32)


def dot_tn(a, b):
    return lax.dot_general(a, b, (((0,), (0,)), ((), ())), preferred_element_type=F32)


def halves(flow, step, count, pieces):
    if step < count // 2 - 1:
        return tuple(range(pieces))
    return tuple(range(pieces // 2)) if flow == 0 else tuple(range(pieces // 2, pieces))


def send_order(flow, step, count, pieces):
    chosen = halves(flow, step, count, pieces)
    if flow == 1 and len(chosen) == pieces:
        chosen = chosen[pieces // 2:] + chosen[:pieces // 2]
    return chosen


def exchange_kernel(
    nx, ny, nt,
    tenant, tok, w, down, up, mag, cot,
    proj_out, gu_out, gd_out, m_out,
    down_v, up_v, mag_v, cot_v, tok_g, w_g, up_sel, up_g, down_sel, cot_l, mag_s, mag_l,
    ex_s, ex_l, rk_s, rk_l, rank_p, parts, sib, ring,
    scaled_s, f_s, f_l, r_s, r_l, h_s, h_l, rank_s, u_s, gu, gd, low_s, proj_s, proj_l, m_s, m_g,
    in_s, tok_ss, tok_rs, w_ss, w_rs, up_ss, up_rs, cot_ss, cot_rs, mag_ss, mag_rs,
    ex_ss, ex_rs, rk_ss, rk_rs, sib_ss, sib_rs, ring_ss, ring_rs, f_ss, f_rs, r_ss, r_rs, h_ss, h_rs,
    u_ss, u_rs, ux_ss, ux_rs, dy_ss, dy_rs, dx_ss, dx_rs, pr_ss, pr_rs, m_ss, m_rs, out_s,
):
    s_per = ny // 2
    nz = nt // 2
    half = nz // 2
    rpy = RANK // ny
    tb, kb = tok.shape
    cb = w.shape[1]
    hb = cb // 2
    dp = lax.axis_index("dp")
    t = lax.axis_index("tensor")
    x, y = lax.div(dp, ny), lax.rem(dp, ny)
    z, core = lax.div(t, 2), lax.rem(t, 2)
    xq, cl = lax.div(t, s_per), lax.rem(t, s_per)
    y_half, y_par = lax.div(y, 2), lax.rem(y, 2)
    at_home = y_half == cl
    away = jnp.logical_not(at_home)
    t_out = s_per * xq + y_half

    def dev(x2, y2, t2):
        return (x2 * ny + y2, t2)

    def wrap(value, count):
        return lax.rem(value + 2 * count, count)

    def on_y(i):
        return dev(x, wrap(y + i, ny), t)

    def on_x(i):
        return dev(wrap(x + i, nx), y, t)

    def on_t(i):
        return dev(x, y, wrap(t + i, nt))

    def on_z(i):
        return dev(x, y, 2 * wrap(z + i, nz) + core)

    def on_swap(p):
        return dev(x, 2 * cl + p, t_out)

    sibling = dev(x, y, 2 * z + 1 - core)
    stays = [jnp.logical_and(at_home, y_par == p) for p in (0, 1)]

    fetches = [
        pltpu.make_async_copy(src, dst, in_s.at[n])
        for n, (src, dst) in enumerate((
            (w, w_g.at[x]), (up, up_v), (down, down_v), (mag, mag_v), (tok, tok_g.at[y]), (cot, cot_v),
        ))
    ]
    for fetch in fetches:
        fetch.start()
    barrier = pltpu.get_barrier_semaphore()

    def greet(device):
        pl.semaphore_signal(barrier, inc=1, device_id=device, device_id_type=pl.DeviceIdType.MESH)

    @pl.loop(1, ny)
    def _(i):
        greet(on_y(i))

    @pl.loop(1, nx)
    def _(i):
        greet(on_x(i))

    @pl.loop(1, nt)
    def _(i):
        greet(on_t(i))

    outs = nx * ny

    def source(i):
        xb, rest = lax.div(i, ny), lax.rem(i, ny)
        return dev(xb, 2 * cl + lax.rem(rest, 2), s_per * xq + lax.div(rest, 2))

    own_source = x * ny + 2 * cl + y_par

    def target(i):
        return (i, t_out)

    @pl.loop(0, outs)
    def _(i):
        @pl.when(jnp.logical_not(jnp.logical_and(at_home, i == own_source)))
        def _():
            greet(source(i))

    for fetch in fetches[1:4]:
        fetch.wait()
    for c in range(nx * s_per):
        up_sel[c // s_per, c % s_per] = up_v[tenant[c]]
    up_g[x] = up_sel[x]
    for c in range(s_per):
        down_sel[c] = down_v[tenant[x * s_per + c]]
    row_ids = lax.broadcasted_iota(jnp.int32, mag_v.shape, 0)
    mag_row = jnp.sum(jnp.where(row_ids == tenant[x * s_per + y_half], mag_v[...], 0.0), axis=0, keepdims=True)
    for p in (0, 1):
        mag_s[p] = jnp.broadcast_to(mag_row[:, p * cb:(p + 1) * cb], (8, cb))

    others = (ny - 1) + (nx - 1) + (nt - 1)

    @pl.when(at_home)
    def _():
        pl.semaphore_wait(barrier, others + outs - 1)

    @pl.when(away)
    def _():
        pl.semaphore_wait(barrier, others + outs)

    pieces = 4
    tp, wp = tb // pieces, kb // pieces

    def sign_of(flow):
        return 1 if flow == 0 else -1

    def tok_copy(flow, step, h):
        sign = sign_of(flow)
        slot = tok_g.at[wrap(y - sign * step, ny), pl.ds(h * tp, tp)]
        src = tok.at[pl.ds(h * tp, tp)] if step == 0 else slot
        return send_to(src, slot, tok_ss.at[flow, step, h], tok_rs.at[flow, step, h], on_y(sign))

    def tok_arrival(flow, step, h):
        sign = sign_of(flow)
        slot = tok_g.at[wrap(y - sign * (step + 1), ny), pl.ds(h * tp, tp)]
        return send_to(slot, slot, tok_ss.at[flow, step, h], tok_rs.at[flow, step, h], on_y(sign))

    def w_copy(flow, step, h):
        sign = sign_of(flow)
        slot = w_g.at[wrap(x - sign * step, nx), pl.ds(h * wp, wp)]
        src = w.at[pl.ds(h * wp, wp)] if step == 0 else slot
        return send_to(src, slot, w_ss.at[flow, step, h], w_rs.at[flow, step, h], on_x(sign))

    def w_arrival(flow, step, h):
        sign = sign_of(flow)
        slot = w_g.at[wrap(x - sign * (step + 1), nx), pl.ds(h * wp, wp)]
        return send_to(slot, slot, w_ss.at[flow, step, h], w_rs.at[flow, step, h], on_x(sign))

    def up_copy(i):
        return send_to(up_sel.at[wrap(x + i, nx)], up_g.at[x], up_ss.at[i], up_rs.at[i], on_x(i))

    def up_arrival(i):
        slot = up_g.at[wrap(x - i, nx)]
        return send_to(slot, slot, up_ss.at[i], up_rs.at[i], on_x(i))

    for place in range(pieces):
        for flow in (0, 1):
            order = send_order(flow, 0, ny, pieces)
            if place < len(order):
                tok_copy(flow, 0, order[place]).start()
            order = send_order(flow, 0, nx, pieces)
            if place < len(order):
                w_copy(flow, 0, order[place]).start()
        if place == 0:
            for i in range(1, nx):
                up_copy(i).start()

    def cot_copy(p):
        return send_to(cot_v.at[:, pl.ds(p * cb, cb)], cot_l.at[y_par], cot_ss.at[p], cot_rs.at[y_par], on_swap(p))

    def cot_arrival(p):
        return send_to(cot_l.at[p], cot_l.at[p], cot_ss.at[p], cot_rs.at[p], on_swap(p))

    def mag_copy(p):
        return send_to(mag_s.at[p], mag_l.at[y_par], mag_ss.at[p], mag_rs.at[y_par], on_swap(p))

    def mag_arrival(p):
        return send_to(mag_l.at[p], mag_l.at[p], mag_ss.at[p], mag_rs.at[p], on_swap(p))

    def send_cot():
        fetches[5].wait()
        for p in (0, 1):
            @pl.when(jnp.logical_not(stays[p]))
            def _():
                cot_copy(p).start()
                mag_copy(p).start()

            @pl.when(stays[p])
            def _():
                cot_l[p] = cot_v[:, p * cb:(p + 1) * cb]
                mag_l[p] = mag_s[p]

    def rank_of(block):
        rank_p[block] = dot_nt(down_sel[lax.div(block, 2)], tok_g[block])

    def squares_of(xb):
        block = w_g[xb]
        block_f32 = block.astype(F32)
        base = jnp.sum(block_f32 * block_f32, axis=0, keepdims=True)
        crossed = dot_nn(down_sel[...].reshape(s_per * RANK, kb), block)
        for c in range(s_per):
            rows = up_g[xb, c]
            quad = dot_tn(grams[c], jnp.concatenate([rows, rows, rows], axis=0))
            mixed = rows.astype(F32) * (2.0 * crossed[c * RANK:(c + 1) * RANK] + quad)
            squares = base + jnp.sum(mixed, axis=0, keepdims=True)
            ex_s[xb * s_per + c, 0:1, :] = squares[:, :hb]
            ex_s[xb * s_per + c, 1:2, :] = squares[:, hb:]

    def ex_copy(i):
        return send_to(ex_s.at[wrap(t + i, nt)], ex_l.at[t], ex_ss.at[i], ex_rs.at[i], on_t(i))

    def ex_arrival(i):
        slot = ex_l.at[wrap(t - i, nt)]
        return send_to(slot, slot, ex_ss.at[i], ex_rs.at[i], on_t(i))

    def rk_copy(i):
        return send_to(rk_s.at[lax.rem(wrap(t + i, nt), s_per)], rk_l.at[t], rk_ss.at[i], rk_rs.at[i], on_t(i))

    def rk_arrival(i):
        slot = rk_l.at[wrap(t - i, nt)]
        return send_to(slot, slot, rk_ss.at[i], rk_rs.at[i], on_t(i))

    def send_ex():
        @pl.loop(1, nt)
        def _(i):
            ex_copy(i).start()

        ex_l[t] = ex_s[t]

    def send_rk():
        for c in range(s_per):
            for p in (0, 1):
                own = rank_p[2 * c + p]
                picked = own[0:rpy]
                for y2 in range(1, ny):
                    picked = jnp.where(y == y2, own[y2 * rpy:(y2 + 1) * rpy], picked)
                rk_s[c, p * rpy:(p + 1) * rpy, :] = picked

        @pl.loop(1, nt)
        def _(i):
            rk_copy(i).start()

        rk_l[t] = rk_s[cl]

    grams = []
    for c in range(s_per):
        rows = down_sel[c]
        grams.append(jnp.concatenate(split3(dot_nt(rows, rows)), axis=0))
    fetches[0].wait()
    squares_of(x)
    fetches[4].wait()
    rank_of(y)

    events = []
    for flow in (0, 1):
        for step in range(ny // 2):
            for n, h in enumerate(send_order(flow, step, ny, pieces)):
                events.append((2.65 + 2.65 * step + 0.65 * n, 0, flow, step, h))
        for step in range(nx // 2):
            for n, h in enumerate(send_order(flow, step, nx, pieces)):
                events.append((3.3 + 5.2 * step + 1.3 * n, 1, flow, step, h))
    events.sort()
    last = {}
    for n, (_, kind, flow, step, h) in enumerate(events):
        last[kind, step] = n
    cot_at = last[0, max(ny // 2 - 2, 0)]
    for n, (_, kind, flow, step, h) in enumerate(events):
        arrival, copy, count = (tok_arrival, tok_copy, ny) if kind == 0 else (w_arrival, w_copy, nx)
        arrival(flow, step, h).wait_recv()
        if step + 1 < count // 2 and h in halves(flow, step + 1, count, pieces):
            copy(flow, step + 1, h).start()
        if n == cot_at:
            send_cot()
        if n == last[kind, step]:
            if kind == 0:
                rank_of(wrap(y + step + 1, ny))
                if step + 1 < ny // 2:
                    rank_of(wrap(y - step - 1, ny))
            else:
                if step == 0:
                    for i in range(1, nx):
                        up_arrival(i).wait_recv()
                squares_of(wrap(x + step + 1, nx))
                if step + 1 < nx // 2:
                    squares_of(wrap(x - step - 1, nx))
                if step + 1 == nx // 2:
                    send_ex()

    def stretch_tokens(c):
        return tok_g[pl.ds(2 * c, 2)].reshape(2 * tb, kb)

    def place_of(i):
        return wrap(z + half + (1 - 2 * lax.rem(i, 2)) * lax.div(i + 1, 2), nz)

    def product(slot):
        xb, c = lax.div(slot, s_per), lax.rem(slot, s_per)
        result = dot_nn(stretch_tokens(c), w_g[xb])
        for p in (0, 1):
            for j in (0, 1):
                parts[slot, 2 * p + j] = result[p * tb:(p + 1) * tb, j * hb:(j + 1) * hb]

    def sib_copy(i):
        zb = place_of(i)
        return send_to(parts.at[2 * zb + 1 - core], sib.at[zb], sib_ss.at[i], sib_rs.at[i], sibling)

    def sib_arrival(i):
        slot = sib.at[place_of(i)]
        return send_to(slot, slot, sib_ss.at[i], sib_rs.at[i], sibling)

    def products(first, end):
        @pl.loop(first, end)
        def _(i):
            product(2 * place_of(i) + 1 - core)
            sib_copy(i).start()
            product(2 * place_of(i) + core)

    def ring_copy(flow, step, q):
        sign = sign_of(flow)
        zb = wrap(z + sign * (half - step), nz)
        return send_to(
            parts.at[2 * zb + core, q], ring.at[flow, step, q],
            ring_ss.at[flow, step, q], ring_rs.at[flow, step, q], on_z(sign),
        )

    def ring_has(flow, step, q):
        return step > 0 or q // 2 == flow

    def ring_send(flow, step, q):
        zb = wrap(z + sign_of(flow) * (half - step), nz)
        value = parts[2 * zb + core, q] + sib[zb, q]
        if step > 0 and ring_has(flow, step - 1, q):
            ring_copy(flow, step - 1, q).wait_recv()
            value = value + ring[flow, step - 1, q]
        parts[2 * zb + core, q] = value
        ring_copy(flow, step, q).start()

    ring_order = ((2, 3, 0, 1), (0, 1, 2, 3))

    def ring_start():
        sib_arrival(0).wait_recv()
        for n in (2, 3):
            for flow in (0, 1):
                ring_send(flow, 0, ring_order[flow][n])

    def ring_step(step, n):
        if n == 0:
            sib_arrival(2 * step - 1).wait_recv()
            sib_arrival(2 * step).wait_recv()
        for flow in (0, 1):
            ring_send(flow, step, ring_order[flow][n])

    norms = {}

    def after_ex():
        @pl.loop(1, nt)
        def _(i):
            ex_arrival(i).wait_recv()

        for p in (0, 1):
            @pl.when(jnp.logical_not(stays[p]))
            def _():
                cot_arrival(p).wait_recv()
                mag_arrival(p).wait_recv()

        total = jnp.sum(ex_l[...], axis=0)
        squares = jnp.concatenate([total[0:1], total[1:2]], axis=1)
        norm = jnp.sqrt(squares + 1e-06)
        scaling = mag_l[0][0:1] / norm
        scaled = cot_l[...].reshape(2 * tb, cb).astype(F32) * scaling
        scaled_s[...] = scaled
        rows = up_g[xq, cl]
        parts3 = split3(scaled)
        back = dot_nt(rows, parts3[0]) + (dot_nt(rows, parts3[1]) + dot_nt(rows, parts3[2]))
        for y2 in range(ny):
            f_s[y2, 0:rpy, :] = back[y2 * rpy:(y2 + 1) * rpy, :tb]
            f_s[y2, rpy:2 * rpy, :] = back[y2 * rpy:(y2 + 1) * rpy, tb:]

        @pl.loop(1, ny)
        def _(i):
            f_copy(i).start()

        f_l[y] = f_s[y]
        norms["norm"], norms["scaling"] = norm, scaling

    def f_copy(i):
        return send_to(f_s.at[wrap(y + i, ny)], f_l.at[y], f_ss.at[i], f_rs.at[i], on_y(i))

    def f_arrival(i):
        slot = f_l.at[wrap(y - i, ny)]
        return send_to(slot, slot, f_ss.at[i], f_rs.at[i], on_y(i))

    def r_copy(i):
        return send_to(r_s, r_l.at[y], r_ss.at[i], r_rs.at[i], on_y(i))

    def r_arrival(i):
        slot = r_l.at[wrap(y - i, ny)]
        return send_to(slot, slot, r_ss.at[i], r_rs.at[i], on_y(i))

    def h_copy(i):
        return send_to(h_s, h_l.at[t], h_ss.at[i], h_rs.at[i], on_t(i))

    def h_arrival(i):
        slot = h_l.at[wrap(t - i, nt)]
        return send_to(slot, slot, h_ss.at[i], h_rs.at[i], on_t(i))

    def after_rk():
        @pl.loop(1, nt)
        def _(i):
            rk_arrival(i).wait_recv()

        r_s[...] = jnp.sum(rk_l[...], axis=0)

        @pl.loop(1, ny)
        def _(i):
            r_copy(i).start()

        r_l[y] = r_s[...]

    def after_f():
        @pl.loop(1, ny)
        def _(i):
            f_arrival(i).wait_recv()

        h_s[...] = jnp.sum(f_l[...], axis=0)

        @pl.loop(1, nt)
        def _(i):
            h_copy(i).start()

        h_l[t] = h_s[...]

    def u_copy(y2):
        return send_to(u_s, gu.at[x, cl, y_par], u_ss.at[y2], u_rs.at[cl, y_par], dev(x, y2, t_out))

    def u_arrival(c, p):
        slot = gu.at[x, c, p]
        return send_to(slot, slot, u_ss.at[0], u_rs.at[c, p], on_swap(p))

    def after_r():
        @pl.loop(1, ny)
        def _(i):
            r_arrival(i).wait_recv()

        for y2 in range(ny):
            rank_s[y2 * rpy:(y2 + 1) * rpy, :tb] = r_l[y2, 0:rpy, :]
            rank_s[y2 * rpy:(y2 + 1) * rpy, tb:] = r_l[y2, rpy:2 * rpy, :]
        a1, a2, a3 = split3(rank_s[...])
        b1, b2, b3 = split3(scaled_s[...])
        low = dot_nn(a3, b1) + dot_nn(a2, b2) + dot_nn(a1, b3)
        u_s[...] = dot_nn(a1, b1) + (dot_nn(a2, b1) + dot_nn(a1, b2) + low)

        @pl.loop(0, ny)
        def _(y2):
            @pl.when(jnp.logical_not(jnp.logical_and(at_home, y2 == y)))
            def _():
                u_copy(y2).start()

        @pl.when(at_home)
        def _():
            gu[x, cl, y_par] = u_s[...]

        rows = up_g[xq, cl]
        low_s[...] = dot_tn(
            jnp.concatenate([a1, a2, a3], axis=0), jnp.concatenate([rows, rows, rows], axis=0)
        )

    def ux_copy(flow, step, h):
        slot = gu.at[wrap(x - sign_of(flow) * step, nx), pl.ds(h * (s_per // 2), s_per // 2)]
        return send_to(slot, slot, ux_ss.at[flow, step, h], ux_rs.at[flow, step, h], on_x(sign_of(flow)))

    def ux_arrival(flow, step, h):
        slot = gu.at[wrap(x - sign_of(flow) * (step + 1), nx), pl.ds(h * (s_per // 2), s_per // 2)]
        return send_to(slot, slot, ux_ss.at[flow, step, h], ux_rs.at[flow, step, h], on_x(sign_of(flow)))

    def dx_copy(flow, step, h):
        slot = gd.at[wrap(x - sign_of(flow) * step, nx), pl.ds(h * (ny // 2), ny // 2)]
        return send_to(slot, slot, dx_ss.at[flow, step, h], dx_rs.at[flow, step, h], on_x(sign_of(flow)))

    def dx_arrival(flow, step, h):
        slot = gd.at[wrap(x - sign_of(flow) * (step + 1), nx), pl.ds(h * (ny // 2), ny // 2)]
        return send_to(slot, slot, dx_ss.at[flow, step, h], dx_rs.at[flow, step, h], on_x(sign_of(flow)))

    def start_x(copy):
        for n in (0, 1):
            for flow in (0, 1):
                order = send_order(flow, 0, nx, 2)
                if n < len(order):
                    copy(flow, 0, order[n]).start()

    def pass_x(copy, arrival, step):
        if step >= nx // 2:
            return
        for n in (0, 1):
            for flow in (0, 1):
                order = send_order(flow, step, nx, 2)
                if n < len(order):
                    arrival(flow, step, order[n]).wait_recv()
                    if step + 1 < nx // 2 and order[n] in halves(flow, step + 1, nx, 2):
                        copy(flow, step + 1, order[n]).start()

    def after_u():
        @pl.loop(0, ny)
        def _(i):
            c, p = lax.div(i, 2), lax.rem(i, 2)

            @pl.when(jnp.logical_not(jnp.logical_and(at_home, i == y)))
            def _():
                u_arrival(c, p).wait_recv()

        start_x(ux_copy)

    def dy_copy(i):
        slot = gd.at[x, y]
        return send_to(slot, slot, dy_ss.at[i], dy_rs.at[i], on_y(i))

    def dy_arrival(i):
        slot = gd.at[x, wrap(y - i, ny)]
        return send_to(slot, slot, dy_ss.at[i], dy_rs.at[i], on_y(i))

    def after_h():
        @pl.loop(1, nt)
        def _(i):
            h_arrival(i).wait_recv()

        for c in range(s_per):
            tile = h_l[c]
            for xb in range(1, nx):
                tile = tile + h_l[xb * s_per + c]
            tile = jnp.concatenate([tile, jnp.zeros((8 - 2 * rpy, tb), F32)], axis=0) if rpy < 4 else tile
            stacked = jnp.concatenate([v.astype(F32) for v in split3(tile)] + [jnp.zeros_like(tile)], axis=0)
            stacked = stacked.astype(BF16)
            both = []
            for p in (0, 1):
                full = dot_nn(stacked, tok_g[2 * c + p])
                both.append(full[0:8] + (full[8:16] + full[16:24]))
            gd[x, y, c * rpy:(c + 1) * rpy, :] = both[0][0:rpy] + both[1][rpy:2 * rpy]

        @pl.loop(1, ny)
        def _(i):
            dy_copy(i).start()

    def after_dy():
        @pl.loop(1, ny)
        def _(i):
            dy_arrival(i).wait_recv()

        start_x(dx_copy)

    products(0, min(3, nz))
    send_rk()
    after_ex()
    ring_start()
    plan = []
    if half > 1:
        plan += [(0.1, lambda: ring_step(1, 0)), (0.2, lambda: ring_step(1, 1))]
        plan += [(3.3, lambda: ring_step(1, 2)), (4.6, lambda: ring_step(1, 3))]
    for step in range(2, half):
        for n in range(4):
            plan.append((5.9 + 5.2 * (step - 2) + 1.3 * n, functools.partial(ring_step, step, n)))
    plan += [
        (0.3, lambda: products(min(3, nz), nz)),
        (2.2, after_rk),
        (3.0, after_f),
        (4.0, after_r),
        (6.0, after_h),
        (8.4, after_u),
        (10.6, after_dy),
        (13.0, lambda: pass_x(ux_copy, ux_arrival, 0)),
        (15.2, lambda: pass_x(dx_copy, dx_arrival, 0)),
        (16.5, lambda: pass_x(ux_copy, ux_arrival, 1)),
    ]
    plan.sort(key=lambda item: item[0])
    for _, action in plan:
        action()
    gu_write = pltpu.make_async_copy(gu, gu_out, out_s.at[0])
    gu_write.start()

    norm, scaling = norms["norm"], norms["scaling"]

    def pr_copy(p, j):
        return send_to(proj_s.at[p, j], proj_l.at[y_par, j], pr_ss.at[p, j], pr_rs.at[y_par, j], on_swap(p))

    def pr_arrival(p, j):
        return send_to(proj_l.at[p, j], proj_l.at[p, j], pr_ss.at[p, j], pr_rs.at[p, j], on_swap(p))

    sib_arrival(nz - 1).wait_recv()
    mag_sum = [None, None]
    for n in range(4):
        for flow in (0, 1):
            q = ring_order[flow][n]
            if ring_has(flow, half - 1, q):
                ring_copy(flow, half - 1, q).wait_recv()
        for q in ([0, 2] if n == 2 else [1, 3] if n == 3 else []):
            p, j = q // 2, q % 2
            lanes = slice(j * hb, (j + 1) * hb)
            value = parts[t, q] + sib[z, q]
            for flow in (0, 1):
                if ring_has(flow, half - 1, q):
                    value = value + ring[flow, half - 1, q]
            value = value + low_s[p * tb:(p + 1) * tb, lanes]
            proj_s[p, j] = (value * scaling[:, lanes]).astype(BF16)

            @pl.when(jnp.logical_not(stays[p]))
            def _():
                pr_copy(p, j).start()

            @pl.when(stays[p])
            def _():
                proj_l[p, j] = proj_s[p, j]

            term = jnp.sum(cot_l[p, :, lanes].astype(F32) * value, axis=0, keepdims=True)
            mag_sum[j] = term if mag_sum[j] is None else mag_sum[j] + term

    for j in (0, 1):
        m_s[j:j + 1, :] = mag_sum[j] / norm[:, j * hb:(j + 1) * hb]

    def m_copy(i):
        return send_to(m_s, m_g.at[x, cl, y_par], m_ss.at[i], m_rs.at[x, cl, y_par], target(i))

    def m_arrival(i):
        xb, rest = lax.div(i, ny), lax.rem(i, ny)
        c, p = lax.div(rest, 2), lax.rem(rest, 2)
        slot = m_g.at[xb, c, p]
        return send_to(slot, slot, m_ss.at[i], m_rs.at[xb, c, p], target(i))

    def not_self(i):
        return jnp.logical_not(jnp.logical_and(at_home, i == dp))

    @pl.loop(0, outs)
    def _(i):
        @pl.when(not_self(i))
        def _():
            m_copy(i).start()

    @pl.when(at_home)
    def _():
        m_g[x, cl, y_par] = m_s[...]

    pass_x(dx_copy, dx_arrival, 1)
    gd_write = pltpu.make_async_copy(gd, gd_out, out_s.at[1])
    gd_write.start()

    def proj_write(p, j):
        return pltpu.make_async_copy(
            proj_l.at[p, j], proj_out.at[:, pl.ds(p * cb + j * hb, hb)], out_s.at[2 + 2 * p + j]
        )

    for flow in (0, 1):
        for step in range(ny // 2):
            for h in halves(flow, step, ny, pieces):
                tok_copy(flow, step, h).wait_send()
        for step in range(nx // 2):
            for h in halves(flow, step, nx, pieces):
                w_copy(flow, step, h).wait_send()
            for h in halves(flow, step, nx, 2):
                ux_copy(flow, step, h).wait_send()
                dx_copy(flow, step, h).wait_send()
        for step in range(half):
            for q in range(4):
                if ring_has(flow, step, q):
                    ring_copy(flow, step, q).wait_send()

    @pl.loop(1, nt)
    def _(i):
        ex_copy(i).wait_send()
        rk_copy(i).wait_send()
        h_copy(i).wait_send()

    @pl.loop(0, nz)
    def _(i):
        sib_copy(i).wait_send()

    @pl.loop(1, ny)
    def _(i):
        f_copy(i).wait_send()
        r_copy(i).wait_send()
        dy_copy(i).wait_send()

    @pl.loop(0, ny)
    def _(y2):
        @pl.when(jnp.logical_not(jnp.logical_and(at_home, y2 == y)))
        def _():
            u_copy(y2).wait_send()

    for i in range(1, nx):
        up_copy(i).wait_send()
    for p in (0, 1):
        @pl.when(jnp.logical_not(stays[p]))
        def _():
            cot_copy(p).wait_send()
            mag_copy(p).wait_send()

    for p in (0, 1):
        for j in (0, 1):
            @pl.when(jnp.logical_not(stays[p]))
            def _():
                pr_arrival(p, j).wait_recv()
                pr_copy(p, j).wait_send()

            proj_write(p, j).start()

    @pl.loop(0, outs)
    def _(i):
        @pl.when(not_self(i))
        def _():
            m_arrival(i).wait_recv()
            m_copy(i).wait_send()

    m_write = pltpu.make_async_copy(m_g, m_out, out_s.at[6])
    m_write.start()
    gu_write.wait()
    gd_write.wait()
    for p in (0, 1):
        for j in (0, 1):
            proj_write(p, j).wait()
    m_write.wait()


def scatter_kernel(nx, ny, tenant, proj, gu_in, gd_in, m_in, proj_out, down_out, up_out, mag_out, gu, gd, m, sems):
    s_per = ny // 2
    rpy = RANK // ny
    copies = [
        pltpu.make_async_copy(src, dst, sems.at[n])
        for n, (src, dst) in enumerate(((gu_in, gu), (gd_in, gd), (m_in, m), (proj, proj_out)))
    ]
    for copy in copies:
        copy.start()
    down_out[...] = jnp.zeros_like(down_out)
    up_out[...] = jnp.zeros_like(up_out)
    for copy in copies:
        copy.wait()
    hb = m.shape[4]
    row_ids = lax.broadcasted_iota(jnp.int32, (mag_out.shape[0], hb), 0)
    mag_sums = [jnp.zeros(row_ids.shape, F32)] * 4
    for xb in range(nx):
        for c in range(s_per):
            who = tenant[xb * s_per + c]
            for p in (0, 1):
                up_out[who, :, 2 * hb * p:2 * hb * (p + 1)] += gu[xb, c, p]
                for j in (0, 1):
                    row = m[xb, c, p, j:j + 1, :]
                    mag_sums[2 * p + j] = mag_sums[2 * p + j] + jnp.where(row_ids == who, row, 0.0)
            rows = [gd[xb, yb, c * rpy:(c + 1) * rpy, :] for yb in range(ny)]
            down_out[who] += jnp.concatenate(rows, axis=0)
    for q in range(4):
        mag_out[:, hb * q:hb * (q + 1)] = mag_sums[q]


def per_device(nx, ny, nt, tokens, base_weight, adapter_down, adapter_up, magnitude, tenant, cotangent):
    tb, kb = tokens.shape
    cb = base_weight.shape[1]
    hb = cb // 2
    tenants = adapter_down.shape[0]
    s_per = ny // 2
    nz = nt // 2
    rpy = RANK // ny
    dma = pltpu.SemaphoreType.DMA
    vmem = pl.BlockSpec(memory_space=pltpu.VMEM)
    smem = pl.BlockSpec(memory_space=pltpu.SMEM)
    hbm = pl.BlockSpec(memory_space=pltpu.HBM)
    scratch = [
        pltpu.VMEM(adapter_down.shape, BF16),
        pltpu.VMEM(adapter_up.shape, BF16),
        pltpu.VMEM(magnitude.shape, F32),
        pltpu.VMEM(cotangent.shape, BF16),
        pltpu.VMEM((ny, tb, kb), BF16),
        pltpu.VMEM((nx, kb, cb), BF16),
        pltpu.VMEM((nx, s_per, RANK, cb), BF16),
        pltpu.VMEM((nx, s_per, RANK, cb), BF16),
        pltpu.VMEM((s_per, RANK, kb), BF16),
        pltpu.VMEM((2, tb, cb), BF16),
        pltpu.VMEM((2, 8, cb), F32),
        pltpu.VMEM((2, 8, cb), F32),
        pltpu.VMEM((nt, 2, hb), F32),
        pltpu.VMEM((nt, 2, hb), F32),
        pltpu.VMEM((s_per, 2 * rpy, tb), F32),
        pltpu.VMEM((nt, 2 * rpy, tb), F32),
        pltpu.VMEM((ny, RANK, tb), F32),
        pltpu.VMEM((nt, 4, tb, hb), F32),
        pltpu.VMEM((nz, 4, tb, hb), F32),
        pltpu.VMEM((2, nz // 2, 4, tb, hb), F32),
        pltpu.VMEM((2 * tb, cb), F32),
        pltpu.VMEM((ny, 2 * rpy, tb), F32),
        pltpu.VMEM((ny, 2 * rpy, tb), F32),
        pltpu.VMEM((2 * rpy, tb), F32),
        pltpu.VMEM((ny, 2 * rpy, tb), F32),
        pltpu.VMEM((2 * rpy, tb), F32),
        pltpu.VMEM((nt, 2 * rpy, tb), F32),
        pltpu.VMEM((RANK, 2 * tb), F32),
        pltpu.VMEM((RANK, cb), F32),
        pltpu.VMEM((nx, s_per, 2, RANK, cb), F32),
        pltpu.VMEM((nx, ny, s_per * rpy, kb), F32),
        pltpu.VMEM((2 * tb, cb), F32),
        pltpu.VMEM((2, 2, tb, hb), BF16),
        pltpu.VMEM((2, 2, tb, hb), BF16),
        pltpu.VMEM((2, hb), F32),
        pltpu.VMEM((nx, s_per, 2, 2, hb), F32),
        dma((6,)),
    ]
    pairs = [
        ((2, ny // 2, 4),) * 2, ((2, nx // 2, 4),) * 2, ((nx,),) * 2, ((2,),) * 2, ((2,),) * 2,
        ((nt,),) * 2, ((nt,),) * 2, ((nz,),) * 2, ((2, nz // 2, 4),) * 2,
        ((ny,),) * 2, ((ny,),) * 2, ((nt,),) * 2,
        ((ny,), (s_per, 2)), ((2, nx // 2, 2),) * 2, ((ny,),) * 2, ((2, nx // 2, 2),) * 2,
        ((2, 2),) * 2, ((nx * ny,), (nx, s_per, 2)),
    ]
    for first, second in pairs:
        scratch += [dma(first), dma(second)]
    scratch.append(dma((7,)))
    proj, up_terms, down_terms, mags = pl.pallas_call(
        functools.partial(exchange_kernel, nx, ny, nt),
        out_shape=(
            jax.ShapeDtypeStruct((tb, 2 * cb), BF16),
            jax.ShapeDtypeStruct((nx, s_per, 2, RANK, cb), F32),
            jax.ShapeDtypeStruct((nx, ny, s_per * rpy, kb), F32),
            jax.ShapeDtypeStruct((nx, s_per, 2, 2, hb), F32),
        ),
        in_specs=[smem] + [hbm] * 6,
        out_specs=(hbm,) * 4,
        scratch_shapes=scratch,
        compiler_params=pltpu.CompilerParams(
            collective_id=0, has_side_effects=True, vmem_limit_bytes=60 * 1024 * 1024
        ),
        name="exchange",
    )(tenant, tokens, base_weight, adapter_down, adapter_up, magnitude, cotangent)
    return pl.pallas_call(
        functools.partial(scatter_kernel, nx, ny),
        out_shape=(
            jax.ShapeDtypeStruct((tb, 2 * cb), BF16),
            jax.ShapeDtypeStruct((tenants, RANK, kb), F32),
            jax.ShapeDtypeStruct((tenants, RANK, 2 * cb), F32),
            jax.ShapeDtypeStruct((tenants, 2 * cb), F32),
        ),
        in_specs=[smem] + [hbm] * 4,
        out_specs=(hbm, vmem, vmem, vmem),
        scratch_shapes=[
            pltpu.VMEM(up_terms.shape, F32),
            pltpu.VMEM(down_terms.shape, F32),
            pltpu.VMEM(mags.shape, F32),
            dma((4,)),
        ],
        compiler_params=pltpu.CompilerParams(vmem_limit_bytes=60 * 1024 * 1024),
        name="scatter",
    )(tenant, proj, up_terms, down_terms, mags)


def solution(mesh, nx=X_CHIPS):
    ny = mesh.shape["dp"] // nx
    nt = mesh.shape["tensor"]
    in_specs = (
        P("dp", "tensor"),
        P("tensor", "dp"),
        P(None, None, "tensor"),
        P(None, None, "dp"),
        P(None, "tensor"),
        P(),
        P("dp", "tensor"),
    )
    out_specs = (
        P("dp", "tensor"),
        P(None, None, "tensor"),
        P(None, None, "tensor"),
        P(None, "tensor"),
    )
    return jax.shard_map(
        functools.partial(per_device, nx, ny, nt),
        mesh=mesh, in_specs=in_specs, out_specs=out_specs, check_vma=False,
    )
```

```python
import functools

import jax
import jax.numpy as jnp
from jax import lax
from jax.experimental import pallas as pl
from jax.experimental.pallas import tpu as pltpu
from jax.sharding import PartitionSpec as P

X_CHIPS = 4
RANK = 16
F32 = jnp.float32
BF16 = jnp.bfloat16


def send_to(src, dst, send_sem, recv_sem, device):
    return pltpu.make_async_remote_copy(
        src_ref=src,
        dst_ref=dst,
        send_sem=send_sem,
        recv_sem=recv_sem,
        device_id=device,
        device_id_type=pl.DeviceIdType.MESH,
    )


def split3(value):
    high = value.astype(BF16)
    rest = value - high.astype(F32)
    middle = rest.astype(BF16)
    low = (rest - middle.astype(F32)).astype(BF16)
    return high, middle, low


def dot_nn(a, b):
    return jnp.dot(a, b, preferred_element_type=F32)


def dot_nt(a, b):
    return lax.dot_general(a, b, (((1,), (1,)), ((), ())), preferred_element_type=F32)


def dot_tn(a, b):
    return lax.dot_general(a, b, (((0,), (0,)), ((), ())), preferred_element_type=F32)


def halves(flow, step, count, pieces):
    if step < count // 2 - 1:
        return tuple(range(pieces))
    return tuple(range(pieces // 2)) if flow == 0 else tuple(range(pieces // 2, pieces))


def send_order(flow, step, count, pieces):
    chosen = halves(flow, step, count, pieces)
    if flow == 1 and len(chosen) == pieces:
        chosen = chosen[pieces // 2:] + chosen[:pieces // 2]
    return chosen


def exchange_kernel(
    nx, ny, nt,
    tenant_in, tok, w, down, up, mag, cot,
    proj_out, gu_out, gd_out, m_out,
    tenant, down_v, up_v, mag_v, cot_v, tok_g, w_g, up_sel, up_g, down_sel, cot_l, mag_s, mag_l,
    ex_s, ex_l, rk_s, rk_l, rank_p, parts, sib, ring,
    scaled_s, f_s, f_l, r_s, r_l, h_s, h_l, rank_s, u_s, gu, gd, low_s, proj_s, proj_l, m_s, m_g,
    in_s, tok_ss, tok_rs, w_ss, w_rs, up_ss, up_rs, cot_ss, cot_rs, mag_ss, mag_rs,
    ex_ss, ex_rs, rk_ss, rk_rs, sib_ss, sib_rs, ring_ss, ring_rs, f_ss, f_rs, r_ss, r_rs, h_ss, h_rs,
    u_ss, u_rs, ux_ss, ux_rs, dy_ss, dy_rs, dx_ss, dx_rs, pr_ss, pr_rs, m_ss, m_rs, out_s,
):
    s_per = ny // 2
    nz = nt // 2
    half = nz // 2
    rpy = RANK // ny
    tb, kb = tok.shape
    cb = w.shape[1]
    hb = cb // 2
    dp = lax.axis_index("dp")
    t = lax.axis_index("tensor")
    x, y = lax.div(dp, ny), lax.rem(dp, ny)
    z, core = lax.div(t, 2), lax.rem(t, 2)
    xq, cl = lax.div(t, s_per), lax.rem(t, s_per)
    y_half, y_par = lax.div(y, 2), lax.rem(y, 2)
    at_home = y_half == cl
    away = jnp.logical_not(at_home)
    t_out = s_per * xq + y_half

    def dev(x2, y2, t2):
        return (x2 * ny + y2, t2)

    def wrap(value, count):
        return lax.rem(value + 2 * count, count)

    def on_y(i):
        return dev(x, wrap(y + i, ny), t)

    def on_x(i):
        return dev(wrap(x + i, nx), y, t)

    def on_t(i):
        return dev(x, y, wrap(t + i, nt))

    def on_z(i):
        return dev(x, y, 2 * wrap(z + i, nz) + core)

    def on_swap(p):
        return dev(x, 2 * cl + p, t_out)

    sibling = dev(x, y, 2 * z + 1 - core)
    stays = [jnp.logical_and(at_home, y_par == p) for p in (0, 1)]

    fetches = [
        pltpu.make_async_copy(src, dst, in_s.at[n])
        for n, (src, dst) in enumerate((
            (w, w_g.at[x]), (up, up_v), (down, down_v), (mag, mag_v), (tok, tok_g.at[y]), (cot, cot_v),
            (tenant_in, tenant),
        ))
    ]
    for fetch in fetches:
        fetch.start()
    barrier = pltpu.get_barrier_semaphore()

    def greet(device):
        pl.semaphore_signal(barrier, inc=1, device_id=device, device_id_type=pl.DeviceIdType.MESH)

    @pl.loop(1, ny)
    def _(i):
        greet(on_y(i))

    @pl.loop(1, nx)
    def _(i):
        greet(on_x(i))

    @pl.loop(1, nt)
    def _(i):
        greet(on_t(i))

    outs = nx * ny

    def target(i):
        return (i, t_out)

    for xb in range(nx):
        for c in range(s_per):
            for p in (0, 1):
                maker = dev(xb, 2 * cl + p, s_per * xq + c)

                @pl.when(jnp.logical_not(jnp.logical_and(maker[0] == dp, maker[1] == t)))
                def _():
                    greet(maker)

    for n in (6, 1, 2, 3):
        fetches[n].wait()
    for c in range(nx * s_per):
        up_sel[c // s_per, c % s_per] = up_v[tenant[c]]
    up_g[x] = up_sel[x]
    for c in range(s_per):
        down_sel[c] = down_v[tenant[x * s_per + c]]
    row_ids = lax.broadcasted_iota(jnp.int32, mag_v.shape, 0)
    mag_row = jnp.sum(jnp.where(row_ids == tenant[x * s_per + y_half], mag_v[...], 0.0), axis=0, keepdims=True)
    for p in (0, 1):
        mag_s[p] = jnp.broadcast_to(mag_row[:, p * cb:(p + 1) * cb], (8, cb))

    others = (ny - 1) + (nx - 1) + (nt - 1)

    @pl.when(at_home)
    def _():
        pl.semaphore_wait(barrier, others + outs - 1)

    @pl.when(away)
    def _():
        pl.semaphore_wait(barrier, others + outs)

    pieces = 4
    tp, wp = tb // pieces, kb // pieces

    def sign_of(flow):
        return 1 if flow == 0 else -1

    def at(count, many, flow, step, h):
        before = sum(len(halves(flow, k, count, many)) for k in range(step))
        place = halves(flow, step, count, many).index(h)
        return flow * (count - 1) * many // 2 + before + place

    def tok_copy(flow, step, h):
        sign = sign_of(flow)
        slot = tok_g.at[wrap(y - sign * step, ny), pl.ds(h * tp, tp)]
        src = tok.at[pl.ds(h * tp, tp)] if step == 0 else slot
        return send_to(src, slot, tok_ss, tok_rs.at[at(ny, pieces, flow, step, h)], on_y(sign))

    def tok_arrival(flow, step, h):
        sign = sign_of(flow)
        slot = tok_g.at[wrap(y - sign * (step + 1), ny), pl.ds(h * tp, tp)]
        return send_to(slot, slot, tok_ss, tok_rs.at[at(ny, pieces, flow, step, h)], on_y(sign))

    def w_copy(flow, step, h):
        sign = sign_of(flow)
        slot = w_g.at[wrap(x - sign * step, nx), pl.ds(h * wp, wp)]
        src = w.at[pl.ds(h * wp, wp)] if step == 0 else slot
        return send_to(src, slot, w_ss, w_rs.at[at(nx, pieces, flow, step, h)], on_x(sign))

    def w_arrival(flow, step, h):
        sign = sign_of(flow)
        slot = w_g.at[wrap(x - sign * (step + 1), nx), pl.ds(h * wp, wp)]
        return send_to(slot, slot, w_ss, w_rs.at[at(nx, pieces, flow, step, h)], on_x(sign))

    def up_copy(i):
        return send_to(up_sel.at[wrap(x + i, nx)], up_g.at[x], up_ss, up_rs, on_x(i))

    def up_all():
        slots = up_g.at[pl.ds(0, nx - 1)]
        return send_to(slots, slots, up_ss, up_rs, on_x(1))

    for place in range(pieces):
        for flow in (0, 1):
            order = send_order(flow, 0, ny, pieces)
            if place < len(order):
                tok_copy(flow, 0, order[place]).start()
            order = send_order(flow, 0, nx, pieces)
            if place < len(order):
                w_copy(flow, 0, order[place]).start()
        if place == 0:
            for i in range(1, nx):
                up_copy(i).start()

    def cot_copy(p):
        return send_to(cot_v.at[:, pl.ds(p * cb, cb)], cot_l.at[y_par], cot_ss.at[p], cot_rs.at[y_par], on_swap(p))

    def cot_arrival(p):
        return send_to(cot_l.at[p], cot_l.at[p], cot_ss.at[p], cot_rs.at[p], on_swap(p))

    def mag_copy(p):
        return send_to(mag_s.at[p], mag_l.at[y_par], mag_ss.at[p], mag_rs.at[y_par], on_swap(p))

    def mag_arrival(p):
        return send_to(mag_l.at[p], mag_l.at[p], mag_ss.at[p], mag_rs.at[p], on_swap(p))

    def send_cot():
        fetches[5].wait()
        for p in (0, 1):
            @pl.when(jnp.logical_not(stays[p]))
            def _():
                cot_copy(p).start()
                mag_copy(p).start()

            @pl.when(stays[p])
            def _():
                cot_l[p] = cot_v[:, p * cb:(p + 1) * cb]
                mag_l[p] = mag_s[p]

    def rank_of(block):
        rank_p[block] = dot_nt(down_sel[lax.div(block, 2)], tok_g[block])

    def squares_of(xb):
        block = w_g[xb]
        block_f32 = block.astype(F32)
        base = jnp.sum(block_f32 * block_f32, axis=0, keepdims=True)
        crossed = dot_nn(down_sel[...].reshape(s_per * RANK, kb), block)
        for c in range(s_per):
            rows = up_g[xb, c]
            quad = dot_tn(grams[c], jnp.concatenate([rows, rows, rows], axis=0))
            mixed = rows.astype(F32) * (2.0 * crossed[c * RANK:(c + 1) * RANK] + quad)
            squares = base + jnp.sum(mixed, axis=0, keepdims=True)
            ex_s[xb * s_per + c, 0:1, :] = squares[:, :hb]
            ex_s[xb * s_per + c, 1:2, :] = squares[:, hb:]

    def ex_copy(i):
        return send_to(ex_s.at[wrap(t + i, nt)], ex_l.at[t], ex_ss, ex_rs, on_t(i))

    def ex_all():
        slots = ex_l.at[pl.ds(0, nt - 1)]
        return send_to(slots, slots, ex_ss, ex_rs, on_t(1))

    def rk_copy(i):
        return send_to(rk_s.at[lax.rem(wrap(t + i, nt), s_per)], rk_l.at[t], rk_ss, rk_rs, on_t(i))

    def rk_all():
        slots = rk_l.at[pl.ds(0, nt - 1)]
        return send_to(slots, slots, rk_ss, rk_rs, on_t(1))

    def send_ex():
        @pl.loop(1, nt)
        def _(i):
            ex_copy(i).start()

        ex_l[t] = ex_s[t]

    def send_rk():
        for c in range(s_per):
            for p in (0, 1):
                own = rank_p[2 * c + p]
                picked = own[0:rpy]
                for y2 in range(1, ny):
                    picked = jnp.where(y == y2, own[y2 * rpy:(y2 + 1) * rpy], picked)
                rk_s[c, p * rpy:(p + 1) * rpy, :] = picked

        @pl.loop(1, nt)
        def _(i):
            rk_copy(i).start()

        rk_l[t] = rk_s[cl]

    grams = []
    for c in range(s_per):
        rows = down_sel[c]
        grams.append(jnp.concatenate(split3(dot_nt(rows, rows)), axis=0))
    fetches[0].wait()
    squares_of(x)
    fetches[4].wait()
    rank_of(y)

    events = []
    for flow in (0, 1):
        for step in range(ny // 2):
            for n, h in enumerate(send_order(flow, step, ny, pieces)):
                events.append((2.65 + 2.65 * step + 0.65 * n, 0, flow, step, h))
        for step in range(nx // 2):
            for n, h in enumerate(send_order(flow, step, nx, pieces)):
                events.append((3.3 + 5.2 * step + 1.3 * n, 1, flow, step, h))
    events.sort()
    last = {}
    for n, (_, kind, flow, step, h) in enumerate(events):
        last[kind, step] = n
    cot_at = last[0, max(ny // 2 - 2, 0)]
    for n, (_, kind, flow, step, h) in enumerate(events):
        arrival, copy, count = (tok_arrival, tok_copy, ny) if kind == 0 else (w_arrival, w_copy, nx)
        arrival(flow, step, h).wait_recv()
        if step + 1 < count // 2 and h in halves(flow, step + 1, count, pieces):
            copy(flow, step + 1, h).start()
        if n == cot_at:
            send_cot()
        if n == last[kind, step]:
            if kind == 0:
                rank_of(wrap(y + step + 1, ny))
                if step + 1 < ny // 2:
                    rank_of(wrap(y - step - 1, ny))
            else:
                if step == 0:
                    up_all().wait_recv()
                squares_of(wrap(x + step + 1, nx))
                if step + 1 < nx // 2:
                    squares_of(wrap(x - step - 1, nx))
                if step + 1 == nx // 2:
                    send_ex()

    def stretch_tokens(c):
        return tok_g[pl.ds(2 * c, 2)].reshape(2 * tb, kb)

    def place_of(i):
        return wrap(z + half + (1 - 2 * lax.rem(i, 2)) * lax.div(i + 1, 2), nz)

    def product(slot):
        xb, c = lax.div(slot, s_per), lax.rem(slot, s_per)
        result = dot_nn(stretch_tokens(c), w_g[xb])
        for p in (0, 1):
            for j in (0, 1):
                parts[slot, 2 * p + j] = result[p * tb:(p + 1) * tb, j * hb:(j + 1) * hb]

    def sib_copy(i):
        zb = place_of(i)
        return send_to(parts.at[2 * zb + 1 - core], sib.at[zb], sib_ss, sib_rs.at[i], sibling)

    def sib_arrival(i):
        slot = sib.at[place_of(i)]
        return send_to(slot, slot, sib_ss, sib_rs.at[i], sibling)

    def products(first, end):
        @pl.loop(first, end)
        def _(i):
            product(2 * place_of(i) + 1 - core)
            sib_copy(i).start()
            product(2 * place_of(i) + core)

    def ring_at(flow, step, q):
        return flow * (nz - 1) * 2 + (q % 2 if step == 0 else 2 + 4 * (step - 1) + q)

    def ring_copy(flow, step, q):
        sign = sign_of(flow)
        zb = wrap(z + sign * (half - step), nz)
        return send_to(
            parts.at[2 * zb + core, q], ring.at[flow, step, q],
            ring_ss, ring_rs.at[ring_at(flow, step, q)], on_z(sign),
        )

    def ring_has(flow, step, q):
        return step > 0 or q // 2 == flow

    def ring_send(flow, step, q):
        zb = wrap(z + sign_of(flow) * (half - step), nz)
        value = parts[2 * zb + core, q] + sib[zb, q]
        if step > 0 and ring_has(flow, step - 1, q):
            ring_copy(flow, step - 1, q).wait_recv()
            value = value + ring[flow, step - 1, q]
        parts[2 * zb + core, q] = value
        ring_copy(flow, step, q).start()

    ring_order = ((2, 3, 0, 1), (0, 1, 2, 3))

    def ring_start():
        sib_arrival(0).wait_recv()
        for n in (2, 3):
            for flow in (0, 1):
                ring_send(flow, 0, ring_order[flow][n])

    def ring_step(step, n):
        if n == 0:
            sib_arrival(2 * step - 1).wait_recv()
            sib_arrival(2 * step).wait_recv()
        for flow in (0, 1):
            ring_send(flow, step, ring_order[flow][n])

    norms = {}

    def after_ex():
        ex_all().wait_recv()

        for p in (0, 1):
            @pl.when(jnp.logical_not(stays[p]))
            def _():
                cot_arrival(p).wait_recv()
                mag_arrival(p).wait_recv()

        total = jnp.sum(ex_l[...], axis=0)
        squares = jnp.concatenate([total[0:1], total[1:2]], axis=1)
        norm = jnp.sqrt(squares + 1e-06)
        scaling = mag_l[0][0:1] / norm
        scaled = cot_l[...].reshape(2 * tb, cb).astype(F32) * scaling
        scaled_s[...] = scaled
        rows = up_g[xq, cl]
        parts3 = split3(scaled)
        back = dot_nt(rows, parts3[0]) + (dot_nt(rows, parts3[1]) + dot_nt(rows, parts3[2]))
        for y2 in range(ny):
            f_s[y2, 0:rpy, :] = back[y2 * rpy:(y2 + 1) * rpy, :tb]
            f_s[y2, rpy:2 * rpy, :] = back[y2 * rpy:(y2 + 1) * rpy, tb:]

        @pl.loop(1, ny)
        def _(i):
            f_copy(i).start()

        f_l[y] = f_s[y]
        norms["norm"], norms["scaling"] = norm, scaling

    def f_copy(i):
        return send_to(f_s.at[wrap(y + i, ny)], f_l.at[y], f_ss, f_rs, on_y(i))

    def f_all():
        slots = f_l.at[pl.ds(0, ny - 1)]
        return send_to(slots, slots, f_ss, f_rs, on_y(1))

    def r_copy(i):
        return send_to(r_s, r_l.at[y], r_ss, r_rs, on_y(i))

    def r_all():
        slots = r_l.at[pl.ds(0, ny - 1)]
        return send_to(slots, slots, r_ss, r_rs, on_y(1))

    def h_copy(i):
        return send_to(h_s, h_l.at[t], h_ss, h_rs, on_t(i))

    def h_all():
        slots = h_l.at[pl.ds(0, nt - 1)]
        return send_to(slots, slots, h_ss, h_rs, on_t(1))

    def after_rk():
        rk_all().wait_recv()

        r_s[...] = jnp.sum(rk_l[...], axis=0)

        @pl.loop(1, ny)
        def _(i):
            r_copy(i).start()

        r_l[y] = r_s[...]

    def after_f():
        f_all().wait_recv()

        h_s[...] = jnp.sum(f_l[...], axis=0)

        @pl.loop(1, nt)
        def _(i):
            h_copy(i).start()

        h_l[t] = h_s[...]

    def u_copy(y2):
        return send_to(u_s, gu.at[x, 2 * cl + y_par], u_ss, u_rs, dev(x, y2, t_out))

    def u_all(count):
        slots = gu.at[x, pl.ds(0, count)]
        return send_to(slots, slots, u_ss, u_rs, on_x(1))

    def by_home(wait, count):
        @pl.when(at_home)
        def _():
            wait(count - 1)

        @pl.when(away)
        def _():
            wait(count)

    def after_r():
        r_all().wait_recv()

        for y2 in range(ny):
            rank_s[y2 * rpy:(y2 + 1) * rpy, :tb] = r_l[y2, 0:rpy, :]
            rank_s[y2 * rpy:(y2 + 1) * rpy, tb:] = r_l[y2, rpy:2 * rpy, :]
        a1, a2, a3 = split3(rank_s[...])
        b1, b2, b3 = split3(scaled_s[...])
        low = dot_nn(a3, b1) + dot_nn(a2, b2) + dot_nn(a1, b3)
        u_s[...] = dot_nn(a1, b1) + (dot_nn(a2, b1) + dot_nn(a1, b2) + low)

        @pl.loop(0, ny)
        def _(y2):
            @pl.when(jnp.logical_not(jnp.logical_and(at_home, y2 == y)))
            def _():
                u_copy(y2).start()

        @pl.when(at_home)
        def _():
            gu[x, 2 * cl + y_par] = u_s[...]

        rows = up_g[xq, cl]
        low_s[...] = dot_tn(
            jnp.concatenate([a1, a2, a3], axis=0), jnp.concatenate([rows, rows, rows], axis=0)
        )

    def ux_copy(flow, step, h):
        slot = gu.at[wrap(x - sign_of(flow) * step, nx), pl.ds(h * (ny // 2), ny // 2)]
        return send_to(slot, slot, ux_ss, ux_rs.at[at(nx, 2, flow, step, h)], on_x(sign_of(flow)))

    def ux_arrival(flow, step, h):
        slot = gu.at[wrap(x - sign_of(flow) * (step + 1), nx), pl.ds(h * (ny // 2), ny // 2)]
        return send_to(slot, slot, ux_ss, ux_rs.at[at(nx, 2, flow, step, h)], on_x(sign_of(flow)))

    def dx_copy(flow, step, h):
        slot = gd.at[wrap(x - sign_of(flow) * step, nx), pl.ds(h * (ny // 2), ny // 2)]
        return send_to(slot, slot, dx_ss, dx_rs.at[at(nx, 2, flow, step, h)], on_x(sign_of(flow)))

    def dx_arrival(flow, step, h):
        slot = gd.at[wrap(x - sign_of(flow) * (step + 1), nx), pl.ds(h * (ny // 2), ny // 2)]
        return send_to(slot, slot, dx_ss, dx_rs.at[at(nx, 2, flow, step, h)], on_x(sign_of(flow)))

    def start_x(copy):
        for n in (0, 1):
            for flow in (0, 1):
                order = send_order(flow, 0, nx, 2)
                if n < len(order):
                    copy(flow, 0, order[n]).start()

    def pass_x(copy, arrival, step):
        if step >= nx // 2:
            return
        for n in (0, 1):
            for flow in (0, 1):
                order = send_order(flow, step, nx, 2)
                if n < len(order):
                    arrival(flow, step, order[n]).wait_recv()
                    if step + 1 < nx // 2 and order[n] in halves(flow, step + 1, nx, 2):
                        copy(flow, step + 1, order[n]).start()

    def after_u():
        by_home(lambda count: u_all(count).wait_recv(), ny)
        start_x(ux_copy)

    def dy_copy(i):
        slot = gd.at[x, y]
        return send_to(slot, slot, dy_ss, dy_rs, on_y(i))

    def dy_all():
        slots = gd.at[x, pl.ds(0, ny - 1)]
        return send_to(slots, slots, dy_ss, dy_rs, on_y(1))

    def after_h():
        h_all().wait_recv()

        for c in range(s_per):
            tile = h_l[c]
            for xb in range(1, nx):
                tile = tile + h_l[xb * s_per + c]
            tile = jnp.concatenate([tile, jnp.zeros((8 - 2 * rpy, tb), F32)], axis=0) if rpy < 4 else tile
            stacked = jnp.concatenate([v.astype(F32) for v in split3(tile)] + [jnp.zeros_like(tile)], axis=0)
            stacked = stacked.astype(BF16)
            both = []
            for p in (0, 1):
                full = dot_nn(stacked, tok_g[2 * c + p])
                both.append(full[0:8] + (full[8:16] + full[16:24]))
            gd[x, y, c * rpy:(c + 1) * rpy, :] = both[0][0:rpy] + both[1][rpy:2 * rpy]

        @pl.loop(1, ny)
        def _(i):
            dy_copy(i).start()

    def after_dy():
        dy_all().wait_recv()

        start_x(dx_copy)

    products(0, 1)
    send_rk()
    products(1, min(3, nz))
    ring_start()
    plan = []
    if half > 1:
        plan += [(0.1, lambda: ring_step(1, 0)), (0.2, lambda: ring_step(1, 1))]
        plan += [(3.3, lambda: ring_step(1, 2)), (4.6, lambda: ring_step(1, 3))]
    for step in range(2, half):
        for n in range(4):
            plan.append((5.9 + 5.2 * (step - 2) + 1.3 * n, functools.partial(ring_step, step, n)))
    plan += [
        (0.3, lambda: products(min(3, nz), nz)),
        (1.5, after_ex),
        (2.5, after_rk),
        (4.0, after_f),
        (5.0, after_r),
        (7.5, after_h),
        (9.5, after_u),
        (12.0, after_dy),
        (13.5, lambda: pass_x(ux_copy, ux_arrival, 0)),
        (16.0, lambda: pass_x(dx_copy, dx_arrival, 0)),
        (17.0, lambda: pass_x(ux_copy, ux_arrival, 1)),
    ]
    plan.sort(key=lambda item: item[0])
    for _, action in plan:
        action()
    gu_write = pltpu.make_async_copy(gu, gu_out, out_s.at[0])
    gu_write.start()

    norm, scaling = norms["norm"], norms["scaling"]

    def pr_copy(p, j):
        return send_to(proj_s.at[p, j], proj_l.at[y_par, j], pr_ss.at[p], pr_rs.at[y_par], on_swap(p))

    def pr_all(p):
        return send_to(proj_l.at[p], proj_l.at[p], pr_ss.at[p], pr_rs.at[p], on_swap(p))

    sib_arrival(nz - 1).wait_recv()
    mag_sum = [None, None]
    for n in range(4):
        for flow in (0, 1):
            q = ring_order[flow][n]
            if ring_has(flow, half - 1, q):
                ring_copy(flow, half - 1, q).wait_recv()
        for q in ([0, 2] if n == 2 else [1, 3] if n == 3 else []):
            p, j = q // 2, q % 2
            lanes = slice(j * hb, (j + 1) * hb)
            value = parts[t, q] + sib[z, q]
            for flow in (0, 1):
                if ring_has(flow, half - 1, q):
                    value = value + ring[flow, half - 1, q]
            value = value + low_s[p * tb:(p + 1) * tb, lanes]
            proj_s[p, j] = (value * scaling[:, lanes]).astype(BF16)

            @pl.when(jnp.logical_not(stays[p]))
            def _():
                pr_copy(p, j).start()

            @pl.when(stays[p])
            def _():
                proj_l[p, j] = proj_s[p, j]

            term = jnp.sum(cot_l[p, :, lanes].astype(F32) * value, axis=0, keepdims=True)
            mag_sum[j] = term if mag_sum[j] is None else mag_sum[j] + term

    for j in (0, 1):
        m_s[j:j + 1, :] = mag_sum[j] / norm[:, j * hb:(j + 1) * hb]

    own_m = (x * s_per + cl) * 2 + y_par

    def m_copy(i):
        return send_to(m_s, m_g.at[own_m], m_ss, m_rs, target(i))

    def m_all(count):
        slots = m_g.at[pl.ds(0, count)]
        return send_to(slots, slots, m_ss, m_rs, on_x(1))

    def not_self(i):
        return jnp.logical_not(jnp.logical_and(at_home, i == dp))

    @pl.loop(0, outs)
    def _(i):
        @pl.when(not_self(i))
        def _():
            m_copy(i).start()

    @pl.when(at_home)
    def _():
        m_g[own_m] = m_s[...]

    def proj_write(p, j):
        return pltpu.make_async_copy(
            proj_l.at[p, j], proj_out.at[:, pl.ds(p * cb + j * hb, hb)], out_s.at[2 + 2 * p + j]
        )

    pass_x(dx_copy, dx_arrival, 1)
    gd_write = pltpu.make_async_copy(gd, gd_out, out_s.at[1])
    gd_write.start()

    def left(ref, send_sem, recv_sem):
        send_to(ref, ref, send_sem, recv_sem, on_y(1)).wait_send()

    left(tok_g.at[pl.ds(0, ny - 1)], tok_ss, tok_rs.at[0])
    left(w_g.at[pl.ds(0, nx - 1)], w_ss, w_rs.at[0])
    left(gu.at[pl.ds(0, nx - 1)], ux_ss, ux_rs.at[0])
    left(parts.at[pl.ds(0, nz - 1)], ring_ss, ring_rs.at[0])
    left(parts.at[pl.ds(0, nz)], sib_ss, sib_rs.at[0])
    up_all().wait_send()
    ex_all().wait_send()
    rk_all().wait_send()
    f_all().wait_send()
    r_all().wait_send()
    h_all().wait_send()
    dy_all().wait_send()
    by_home(lambda count: u_all(count).wait_send(), ny)
    for p in (0, 1):
        @pl.when(jnp.logical_not(stays[p]))
        def _():
            cot_copy(p).wait_send()
            mag_copy(p).wait_send()

    for p in (0, 1):
        @pl.when(jnp.logical_not(stays[p]))
        def _():
            pr_all(p).wait_recv()
            pr_all(p).wait_send()

        for j in (0, 1):
            proj_write(p, j).start()

    by_home(lambda count: m_all(count).wait_recv(), outs)
    by_home(lambda count: m_all(count).wait_send(), outs)
    left(gd.at[pl.ds(0, nx - 1)], dx_ss, dx_rs.at[0])
    m_write = pltpu.make_async_copy(m_g, m_out, out_s.at[6])
    m_write.start()
    gu_write.wait()
    gd_write.wait()
    for p in (0, 1):
        for j in (0, 1):
            proj_write(p, j).wait()
    m_write.wait()


def scatter_kernel(
    nx, ny, tenant_in, proj_in, gu_in, gd_in, m_in, proj_out, down_out, up_out, mag_out,
    tenant, proj, gu, gd, m, down, up, mag, sems,
):
    s_per = ny // 2
    rpy = RANK // ny
    hb = m.shape[2]
    cb = 2 * hb
    ins = ((tenant_in, tenant), (gu_in, gu), (gd_in, gd), (m_in, m), (proj_in, proj))
    outs = ((up, up_out), (down, down_out), (mag, mag_out), (proj, proj_out))
    reads = [pltpu.make_async_copy(src, dst, sems.at[n]) for n, (src, dst) in enumerate(ins)]
    writes = [pltpu.make_async_copy(src, dst, sems.at[5 + n]) for n, (src, dst) in enumerate(outs)]
    for read in reads:
        read.start()
    up[...] = jnp.zeros_like(up)
    down[...] = jnp.zeros_like(down)
    reads[0].wait()
    who = [tenant[n] for n in range(nx * s_per)]
    reads[1].wait()
    for n in range(nx * s_per):
        for p in (0, 1):
            up[who[n], :, cb * p:cb * (p + 1)] += gu[n // s_per, 2 * (n % s_per) + p]
    writes[0].start()
    reads[2].wait()
    for n in range(nx * s_per):
        c = n % s_per
        rows = [gd[n // s_per, yb, c * rpy:(c + 1) * rpy, :] for yb in range(ny)]
        down[who[n]] += jnp.concatenate(rows, axis=0)
    writes[1].start()
    reads[4].wait()
    writes[3].start()
    reads[3].wait()
    row_ids = lax.broadcasted_iota(jnp.int32, (mag.shape[0], hb), 0)
    sums = [jnp.zeros(row_ids.shape, F32)] * 4
    for n in range(nx * s_per):
        for q in range(4):
            sums[q] = sums[q] + jnp.where(row_ids == who[n], m[2 * n + q // 2, q % 2:q % 2 + 1, :], 0.0)
    for q in range(4):
        mag[:, hb * q:hb * (q + 1)] = sums[q]
    writes[2].start()
    for write in writes:
        write.wait()


def per_device(nx, ny, nt, tokens, base_weight, adapter_down, adapter_up, magnitude, tenant, cotangent):
    tb, kb = tokens.shape
    cb = base_weight.shape[1]
    hb = cb // 2
    tenants = adapter_down.shape[0]
    s_per = ny // 2
    nz = nt // 2
    rpy = RANK // ny
    dma = pltpu.SemaphoreType.DMA
    vmem = pl.BlockSpec(memory_space=pltpu.VMEM)
    hbm = pl.BlockSpec(memory_space=pltpu.HBM)
    scratch = [
        pltpu.SMEM(tenant.shape, jnp.int32),
        pltpu.VMEM(adapter_down.shape, BF16),
        pltpu.VMEM(adapter_up.shape, BF16),
        pltpu.VMEM(magnitude.shape, F32),
        pltpu.VMEM(cotangent.shape, BF16),
        pltpu.VMEM((ny, tb, kb), BF16),
        pltpu.VMEM((nx, kb, cb), BF16),
        pltpu.VMEM((nx, s_per, RANK, cb), BF16),
        pltpu.VMEM((nx, s_per, RANK, cb), BF16),
        pltpu.VMEM((s_per, RANK, kb), BF16),
        pltpu.VMEM((2, tb, cb), BF16),
        pltpu.VMEM((2, 8, cb), F32),
        pltpu.VMEM((2, 8, cb), F32),
        pltpu.VMEM((nt, 2, hb), F32),
        pltpu.VMEM((nt, 2, hb), F32),
        pltpu.VMEM((s_per, 2 * rpy, tb), F32),
        pltpu.VMEM((nt, 2 * rpy, tb), F32),
        pltpu.VMEM((ny, RANK, tb), F32),
        pltpu.VMEM((nt, 4, tb, hb), F32),
        pltpu.VMEM((nz, 4, tb, hb), F32),
        pltpu.VMEM((2, nz // 2, 4, tb, hb), F32),
        pltpu.VMEM((2 * tb, cb), F32),
        pltpu.VMEM((ny, 2 * rpy, tb), F32),
        pltpu.VMEM((ny, 2 * rpy, tb), F32),
        pltpu.VMEM((2 * rpy, tb), F32),
        pltpu.VMEM((ny, 2 * rpy, tb), F32),
        pltpu.VMEM((2 * rpy, tb), F32),
        pltpu.VMEM((nt, 2 * rpy, tb), F32),
        pltpu.VMEM((RANK, 2 * tb), F32),
        pltpu.VMEM((RANK, cb), F32),
        pltpu.VMEM((nx, ny, RANK, cb), F32),
        pltpu.VMEM((nx, ny, s_per * rpy, kb), F32),
        pltpu.VMEM((2 * tb, cb), F32),
        pltpu.VMEM((2, 2, tb, hb), BF16),
        pltpu.VMEM((2, 2, tb, hb), BF16),
        pltpu.VMEM((2, hb), F32),
        pltpu.VMEM((nx * ny, 2, hb), F32),
        dma((7,)),
    ]
    tok_n, w_n, x_n, ring_n = 4 * (ny - 1), 4 * (nx - 1), 2 * (nx - 1), 4 * (nz - 1)
    pairs = [
        (1, tok_n), (1, w_n), (1, 1), (2, 2), (2, 2), (1, 1), (1, 1), (1, nz), (1, ring_n),
        (1, 1), (1, 1), (1, 1), (1, 1), (1, x_n), (1, 1), (1, x_n), (2, 2), (1, 1),
    ]
    for pair in pairs:
        scratch += [dma if count == 1 else dma((count,)) for count in pair]
    scratch.append(dma((7,)))
    proj, up_terms, down_terms, mags = pl.pallas_call(
        functools.partial(exchange_kernel, nx, ny, nt),
        out_shape=(
            jax.ShapeDtypeStruct((tb, 2 * cb), BF16),
            jax.ShapeDtypeStruct((nx, ny, RANK, cb), F32),
            jax.ShapeDtypeStruct((nx, ny, s_per * rpy, kb), F32),
            jax.ShapeDtypeStruct((nx * ny, 2, hb), F32),
        ),
        in_specs=[hbm] * 7,
        out_specs=(hbm,) * 4,
        scratch_shapes=scratch,
        compiler_params=pltpu.CompilerParams(
            collective_id=0, has_side_effects=True, vmem_limit_bytes=60 * 1024 * 1024
        ),
        name="exchange",
    )(tenant, tokens, base_weight, adapter_down, adapter_up, magnitude, cotangent)
    return pl.pallas_call(
        functools.partial(scatter_kernel, nx, ny),
        out_shape=(
            jax.ShapeDtypeStruct((tb, 2 * cb), BF16),
            jax.ShapeDtypeStruct((tenants, RANK, kb), F32),
            jax.ShapeDtypeStruct((tenants, RANK, 2 * cb), F32),
            jax.ShapeDtypeStruct((tenants, 2 * cb), F32),
        ),
        in_specs=[hbm] * 5,
        out_specs=(hbm,) * 4,
        scratch_shapes=[
            pltpu.SMEM(tenant.shape, jnp.int32),
            pltpu.VMEM(proj.shape, BF16),
            pltpu.VMEM(up_terms.shape, F32),
            pltpu.VMEM(down_terms.shape, F32),
            pltpu.VMEM(mags.shape, F32),
            pltpu.VMEM((tenants, RANK, kb), F32),
            pltpu.VMEM((tenants, RANK, 2 * cb), F32),
            pltpu.VMEM((tenants, 2 * cb), F32),
            dma((9,)),
        ],
        compiler_params=pltpu.CompilerParams(vmem_limit_bytes=60 * 1024 * 1024),
        name="scatter",
    )(tenant, proj, up_terms, down_terms, mags)


def solution(mesh, nx=X_CHIPS):
    ny = mesh.shape["dp"] // nx
    nt = mesh.shape["tensor"]
    in_specs = (
        P("dp", "tensor"),
        P("tensor", "dp"),
        P(None, None, "tensor"),
        P(None, None, "dp"),
        P(None, "tensor"),
        P(),
        P("dp", "tensor"),
    )
    out_specs = (
        P("dp", "tensor"),
        P(None, None, "tensor"),
        P(None, None, "tensor"),
        P(None, "tensor"),
    )
    return jax.shard_map(
        functools.partial(per_device, nx, ny, nt),
        mesh=mesh, in_specs=in_specs, out_specs=out_specs, check_vma=False,
    )
```

```python
import functools

import jax
import jax.numpy as jnp
from jax import lax
from jax.experimental import pallas as pl
from jax.experimental.pallas import tpu as pltpu
from jax.sharding import PartitionSpec as P

X_CHIPS = 4
RANK = 16
F32 = jnp.float32
BF16 = jnp.bfloat16


def send_to(src, dst, send_sem, recv_sem, device):
    return pltpu.make_async_remote_copy(
        src_ref=src,
        dst_ref=dst,
        send_sem=send_sem,
        recv_sem=recv_sem,
        device_id=device,
        device_id_type=pl.DeviceIdType.MESH,
    )


def split3(value):
    high = value.astype(BF16)
    rest = value - high.astype(F32)
    middle = rest.astype(BF16)
    low = (rest - middle.astype(F32)).astype(BF16)
    return high, middle, low


def dot_nn(a, b):
    return jnp.dot(a, b, preferred_element_type=F32)


def dot_nt(a, b):
    return lax.dot_general(a, b, (((1,), (1,)), ((), ())), preferred_element_type=F32)


def dot_tn(a, b):
    return lax.dot_general(a, b, (((0,), (0,)), ((), ())), preferred_element_type=F32)


def halves(flow, step, count, pieces):
    if step < count // 2 - 1:
        return tuple(range(pieces))
    return tuple(range(pieces // 2)) if flow == 0 else tuple(range(pieces // 2, pieces))


def send_order(flow, step, count, pieces):
    chosen = halves(flow, step, count, pieces)
    if flow == 1 and len(chosen) == pieces:
        chosen = chosen[pieces // 2:] + chosen[:pieces // 2]
    return chosen


def exchange_kernel(
    nx, ny, nt,
    tenant_in, tok, w, down, up, mag, cot,
    proj_out, gu_out, gd_out, m_out,
    tenant, down_v, up_v, mag_v, cot_v, tok_g, w_g, up_sel, up_g, down_sel, cot_l, mag_s, mag_l,
    ex_s, ex_l, rk_s, rk_l, rank_p, parts, sib, ring,
    scaled_s, f_s, f_l, r_s, r_l, h_s, h_l, rank_s, u_s, gu, gd, low_s, proj_s, proj_l, m_s, m_g,
    in_s, tok_ss, tok_rs, w_ss, w_rs, up_ss, up_rs, cot_ss, cot_rs, mag_ss, mag_rs,
    ex_ss, ex_rs, rk_ss, rk_rs, sib_ss, sib_rs, first_rs, ring_ss, ring_rs, f_ss, f_rs, r_ss, r_rs, h_ss, h_rs,
    u_ss, u_rs, ux_ss, ux_rs, dy_ss, dy_rs, dx_ss, dx_rs, pr_ss, pr_rs, m_ss, m_rs, out_s,
):
    s_per = ny // 2
    nz = nt // 2
    half = nz // 2
    rpy = RANK // ny
    tb, kb = tok.shape
    cb = w.shape[1]
    hb = cb // 2
    dp = lax.axis_index("dp")
    t = lax.axis_index("tensor")
    x, y = lax.div(dp, ny), lax.rem(dp, ny)
    z, core = lax.div(t, 2), lax.rem(t, 2)
    xq, cl = lax.div(t, s_per), lax.rem(t, s_per)
    y_half, y_par = lax.div(y, 2), lax.rem(y, 2)
    at_home = y_half == cl
    away = jnp.logical_not(at_home)
    t_out = s_per * xq + y_half

    def dev(x2, y2, t2):
        return (x2 * ny + y2, t2)

    def wrap(value, count):
        return lax.rem(value + 2 * count, count)

    def on_y(i):
        return dev(x, wrap(y + i, ny), t)

    def on_x(i):
        return dev(wrap(x + i, nx), y, t)

    def on_t(i):
        return dev(x, y, wrap(t + i, nt))

    def on_z(i):
        return dev(x, y, 2 * wrap(z + i, nz) + core)

    def on_swap(p):
        return dev(x, 2 * cl + p, t_out)

    sibling = dev(x, y, 2 * z + 1 - core)
    stays = [jnp.logical_and(at_home, y_par == p) for p in (0, 1)]

    fetches = [
        pltpu.make_async_copy(src, dst, in_s.at[n])
        for n, (src, dst) in enumerate((
            (w, w_g.at[x]), (up, up_v), (down, down_v), (mag, mag_v), (tok, tok_g.at[y]), (cot, cot_v),
            (tenant_in, tenant),
        ))
    ]
    for fetch in fetches:
        fetch.start()
    barrier = pltpu.get_barrier_semaphore()

    def greet(device):
        pl.semaphore_signal(barrier, inc=1, device_id=device, device_id_type=pl.DeviceIdType.MESH)

    @pl.loop(1, ny)
    def _(i):
        greet(on_y(i))

    @pl.loop(1, nx)
    def _(i):
        greet(on_x(i))

    @pl.loop(1, nt)
    def _(i):
        greet(on_t(i))

    outs = nx * ny

    def target(i):
        return (wrap(dp + i, outs), t_out)

    for xb in range(nx):
        for c in range(s_per):
            for p in (0, 1):
                maker = dev(xb, 2 * cl + p, s_per * xq + c)

                @pl.when(jnp.logical_not(jnp.logical_and(maker[0] == dp, maker[1] == t)))
                def _():
                    greet(maker)

    others = (ny - 1) + (nx - 1) + (nt - 1)

    @pl.when(at_home)
    def _():
        pl.semaphore_wait(barrier, others + outs - 1)

    @pl.when(away)
    def _():
        pl.semaphore_wait(barrier, others + outs)

    pieces = 4
    tp, wp = tb // pieces, kb // pieces

    def sign_of(flow):
        return 1 if flow == 0 else -1

    def at(count, many, flow, step, h):
        before = sum(len(halves(flow, k, count, many)) for k in range(step))
        place = halves(flow, step, count, many).index(h)
        return flow * (count - 1) * many // 2 + before + place

    def tok_copy(flow, step, h):
        sign = sign_of(flow)
        slot = tok_g.at[wrap(y - sign * step, ny), pl.ds(h * tp, tp)]
        src = tok.at[pl.ds(h * tp, tp)] if step == 0 else slot
        return send_to(src, slot, tok_ss, tok_rs.at[at(ny, pieces, flow, step, h)], on_y(sign))

    def tok_arrival(flow, step, h):
        sign = sign_of(flow)
        slot = tok_g.at[wrap(y - sign * (step + 1), ny), pl.ds(h * tp, tp)]
        return send_to(slot, slot, tok_ss, tok_rs.at[at(ny, pieces, flow, step, h)], on_y(sign))

    def w_copy(flow, step, h):
        sign = sign_of(flow)
        slot = w_g.at[wrap(x - sign * step, nx), pl.ds(h * wp, wp)]
        src = w.at[pl.ds(h * wp, wp)] if step == 0 else slot
        return send_to(src, slot, w_ss, w_rs.at[at(nx, pieces, flow, step, h)], on_x(sign))

    def w_arrival(flow, step, h):
        sign = sign_of(flow)
        slot = w_g.at[wrap(x - sign * (step + 1), nx), pl.ds(h * wp, wp)]
        return send_to(slot, slot, w_ss, w_rs.at[at(nx, pieces, flow, step, h)], on_x(sign))

    def up_copy(i):
        return send_to(up_sel.at[wrap(x + i, nx)], up_g.at[x], up_ss, up_rs, on_x(i))

    def up_all():
        slots = up_g.at[pl.ds(0, nx - 1)]
        return send_to(slots, slots, up_ss, up_rs, on_x(1))

    for flow in (0, 1):
        tok_copy(flow, 0, send_order(flow, 0, ny, pieces)[0]).start()
        w_copy(flow, 0, send_order(flow, 0, nx, pieces)[0]).start()

    for n in (6, 1, 2, 3):
        fetches[n].wait()
    for c in range(nx * s_per):
        up_sel[c // s_per, c % s_per] = up_v[tenant[c]]
    up_g[x] = up_sel[x]
    for c in range(s_per):
        down_sel[c] = down_v[tenant[x * s_per + c]]
    row_ids = lax.broadcasted_iota(jnp.int32, mag_v.shape, 0)
    mag_row = jnp.sum(jnp.where(row_ids == tenant[x * s_per + y_half], mag_v[...], 0.0), axis=0, keepdims=True)
    for p in (0, 1):
        mag_s[p] = jnp.broadcast_to(mag_row[:, p * cb:(p + 1) * cb], (8, cb))

    for i in range(1, nx):
        up_copy(i).start()

    for place in range(1, pieces):
        for flow in (0, 1):
            order = send_order(flow, 0, ny, pieces)
            if place < len(order):
                tok_copy(flow, 0, order[place]).start()
            order = send_order(flow, 0, nx, pieces)
            if place < len(order):
                w_copy(flow, 0, order[place]).start()

    def cot_copy(p):
        return send_to(cot_v.at[:, pl.ds(p * cb, cb)], cot_l.at[y_par], cot_ss.at[p], cot_rs.at[y_par], on_swap(p))

    def cot_arrival(p):
        return send_to(cot_l.at[p], cot_l.at[p], cot_ss.at[p], cot_rs.at[p], on_swap(p))

    def mag_copy(p):
        return send_to(mag_s.at[p], mag_l.at[y_par], mag_ss.at[p], mag_rs.at[y_par], on_swap(p))

    def mag_arrival(p):
        return send_to(mag_l.at[p], mag_l.at[p], mag_ss.at[p], mag_rs.at[p], on_swap(p))

    def send_cot():
        fetches[5].wait()
        for p in (0, 1):
            @pl.when(jnp.logical_not(stays[p]))
            def _():
                cot_copy(p).start()
                mag_copy(p).start()

            @pl.when(stays[p])
            def _():
                cot_l[p] = cot_v[:, p * cb:(p + 1) * cb]
                mag_l[p] = mag_s[p]

    def rank_of(block):
        rank_p[block] = dot_nt(down_sel[lax.div(block, 2)], tok_g[block])

    def squares_of(xb):
        block = w_g[xb]
        block_f32 = block.astype(F32)
        base = jnp.sum(block_f32 * block_f32, axis=0, keepdims=True)
        crossed = dot_nn(down_sel[...].reshape(s_per * RANK, kb), block)
        for c in range(s_per):
            rows = up_g[xb, c]
            quad = dot_tn(grams[c], jnp.concatenate([rows, rows, rows], axis=0))
            mixed = rows.astype(F32) * (2.0 * crossed[c * RANK:(c + 1) * RANK] + quad)
            squares = base + jnp.sum(mixed, axis=0, keepdims=True)
            ex_s[xb * s_per + c, 0:1, :] = squares[:, :hb]
            ex_s[xb * s_per + c, 1:2, :] = squares[:, hb:]

    def ex_copy(i):
        return send_to(ex_s.at[wrap(t + i, nt)], ex_l.at[t], ex_ss, ex_rs, on_t(i))

    def ex_all():
        slots = ex_l.at[pl.ds(0, nt - 1)]
        return send_to(slots, slots, ex_ss, ex_rs, on_t(1))

    def rk_copy(i):
        return send_to(rk_s.at[lax.rem(wrap(t + i, nt), s_per)], rk_l.at[t], rk_ss, rk_rs, on_t(i))

    def rk_all():
        slots = rk_l.at[pl.ds(0, nt - 1)]
        return send_to(slots, slots, rk_ss, rk_rs, on_t(1))

    def send_ex():
        @pl.loop(1, nt)
        def _(i):
            ex_copy(i).start()

        ex_l[t] = ex_s[t]

    def send_rk():
        for c in range(s_per):
            for p in (0, 1):
                own = rank_p[2 * c + p]
                picked = own[0:rpy]
                for y2 in range(1, ny):
                    picked = jnp.where(y == y2, own[y2 * rpy:(y2 + 1) * rpy], picked)
                rk_s[c, p * rpy:(p + 1) * rpy, :] = picked

        @pl.loop(1, nt)
        def _(i):
            rk_copy(i).start()

        rk_l[t] = rk_s[cl]

    grams = []
    for c in range(s_per):
        rows = down_sel[c]
        grams.append(jnp.concatenate(split3(dot_nt(rows, rows)), axis=0))
    fetches[0].wait()
    squares_of(x)
    fetches[4].wait()
    rank_of(y)

    events = []
    for flow in (0, 1):
        for step in range(ny // 2):
            for n, h in enumerate(send_order(flow, step, ny, pieces)):
                events.append((2.65 + 2.65 * step + 0.65 * n, 0, flow, step, h))
        for step in range(nx // 2):
            for n, h in enumerate(send_order(flow, step, nx, pieces)):
                events.append((3.3 + 5.2 * step + 1.3 * n, 1, flow, step, h))
    events.sort()
    last = {}
    for n, (_, kind, flow, step, h) in enumerate(events):
        last[kind, step] = n
    cot_at = last[0, max(ny // 2 - 2, 0)]
    for n, (_, kind, flow, step, h) in enumerate(events):
        arrival, copy, count = (tok_arrival, tok_copy, ny) if kind == 0 else (w_arrival, w_copy, nx)
        arrival(flow, step, h).wait_recv()
        if step + 1 < count // 2 and h in halves(flow, step + 1, count, pieces):
            copy(flow, step + 1, h).start()
        if n == cot_at:
            send_cot()
        if n == last[kind, step]:
            if kind == 0:
                rank_of(wrap(y + step + 1, ny))
                if step + 1 < ny // 2:
                    rank_of(wrap(y - step - 1, ny))
            else:
                if step == 0:
                    up_all().wait_recv()
                squares_of(wrap(x + step + 1, nx))
                if step + 1 < nx // 2:
                    squares_of(wrap(x - step - 1, nx))
                if step + 1 == nx // 2:
                    send_ex()

    def stretch_tokens(c):
        return tok_g[pl.ds(2 * c, 2)].reshape(2 * tb, kb)

    def place_of(i):
        return wrap(z + half + (1 - 2 * lax.rem(i, 2)) * lax.div(i + 1, 2), nz)

    def product(slot):
        xb, c = lax.div(slot, s_per), lax.rem(slot, s_per)
        result = dot_nn(stretch_tokens(c), w_g[xb])
        for p in (0, 1):
            for j in (0, 1):
                parts[slot, 2 * p + j] = result[p * tb:(p + 1) * tb, j * hb:(j + 1) * hb]

    def sib_copy(i):
        zb = place_of(i)
        return send_to(parts.at[2 * zb + 1 - core], sib.at[zb], sib_ss, sib_rs.at[i], sibling)

    def sib_arrival(i):
        slot = sib.at[place_of(i)]
        return send_to(slot, slot, sib_ss, sib_rs.at[i], sibling)

    def first_copy(q):
        zb = place_of(0)
        return send_to(parts.at[2 * zb + 1 - core, q], sib.at[zb, q], sib_ss, first_rs.at[q], sibling)

    def products(first, end):
        @pl.loop(first, end)
        def _(i):
            product(2 * place_of(i) + 1 - core)
            sib_copy(i).start()
            product(2 * place_of(i) + core)

    def ring_at(flow, step, q):
        return flow * (nz - 1) * 2 + (q % 2 if step == 0 else 2 + 4 * (step - 1) + q)

    def ring_copy(flow, step, q):
        sign = sign_of(flow)
        zb = wrap(z + sign * (half - step), nz)
        return send_to(
            parts.at[2 * zb + core, q], ring.at[flow, step, q],
            ring_ss, ring_rs.at[ring_at(flow, step, q)], on_z(sign),
        )

    def ring_has(flow, step, q):
        return step > 0 or q // 2 == flow

    def ring_send(flow, step, q):
        zb = wrap(z + sign_of(flow) * (half - step), nz)
        value = parts[2 * zb + core, q] + sib[zb, q]
        if step > 0 and ring_has(flow, step - 1, q):
            ring_copy(flow, step - 1, q).wait_recv()
            value = value + ring[flow, step - 1, q]
        parts[2 * zb + core, q] = value
        ring_copy(flow, step, q).start()

    ring_order = ((2, 3, 0, 1), (0, 1, 2, 3))

    def order_at(flow, step):
        return ring_order[flow] if step < 2 else (0, 1, 2, 3)


    def ring_start():
        for n in (2, 3):
            for flow in (0, 1):
                q = ring_order[flow][n]
                first_copy(q).wait_recv()
                ring_send(flow, 0, q)

    def ring_step(step, n):
        if n == 0:
            sib_arrival(2 * step - 1).wait_recv()
            sib_arrival(2 * step).wait_recv()
        for flow in (0, 1):
            ring_send(flow, step, order_at(flow, step)[n])

    norms = {}

    def after_ex():
        ex_all().wait_recv()

        for p in (0, 1):
            @pl.when(jnp.logical_not(stays[p]))
            def _():
                cot_arrival(p).wait_recv()
                mag_arrival(p).wait_recv()

        total = jnp.sum(ex_l[...], axis=0)
        squares = jnp.concatenate([total[0:1], total[1:2]], axis=1)
        norm = jnp.sqrt(squares + 1e-06)
        scaling = mag_l[0][0:1] / norm
        scaled = cot_l[...].reshape(2 * tb, cb).astype(F32) * scaling
        scaled_s[...] = scaled
        rows = up_g[xq, cl]
        parts3 = split3(scaled)
        back = dot_nt(rows, parts3[0]) + (dot_nt(rows, parts3[1]) + dot_nt(rows, parts3[2]))
        for y2 in range(ny):
            f_s[y2, 0:rpy, :] = back[y2 * rpy:(y2 + 1) * rpy, :tb]
            f_s[y2, rpy:2 * rpy, :] = back[y2 * rpy:(y2 + 1) * rpy, tb:]

        @pl.loop(1, ny)
        def _(i):
            f_copy(i).start()

        f_l[y] = f_s[y]
        norms["norm"], norms["scaling"] = norm, scaling

    def f_copy(i):
        return send_to(f_s.at[wrap(y + i, ny)], f_l.at[y], f_ss, f_rs, on_y(i))

    def f_all():
        slots = f_l.at[pl.ds(0, ny - 1)]
        return send_to(slots, slots, f_ss, f_rs, on_y(1))

    def r_copy(i):
        return send_to(r_s, r_l.at[y], r_ss, r_rs, on_y(i))

    def r_all():
        slots = r_l.at[pl.ds(0, ny - 1)]
        return send_to(slots, slots, r_ss, r_rs, on_y(1))

    def h_copy(i):
        return send_to(h_s, h_l.at[t], h_ss, h_rs, on_t(i))

    def h_all():
        slots = h_l.at[pl.ds(0, nt - 1)]
        return send_to(slots, slots, h_ss, h_rs, on_t(1))

    def after_rk():
        rk_all().wait_recv()

        r_s[...] = jnp.sum(rk_l[...], axis=0)

        @pl.loop(1, ny)
        def _(i):
            r_copy(i).start()

        r_l[y] = r_s[...]

    def after_f():
        f_all().wait_recv()

        h_s[...] = jnp.sum(f_l[...], axis=0)

        @pl.loop(1, nt)
        def _(i):
            h_copy(i).start()

        h_l[t] = h_s[...]

    def u_copy(y2):
        return send_to(u_s, gu.at[x, 2 * cl + y_par], u_ss, u_rs, dev(x, y2, t_out))

    def u_all(count):
        slots = gu.at[x, pl.ds(0, count)]
        return send_to(slots, slots, u_ss, u_rs, on_x(1))

    def by_home(wait, count):
        @pl.when(at_home)
        def _():
            wait(count - 1)

        @pl.when(away)
        def _():
            wait(count)

    def after_r():
        r_all().wait_recv()

        for y2 in range(ny):
            rank_s[y2 * rpy:(y2 + 1) * rpy, :tb] = r_l[y2, 0:rpy, :]
            rank_s[y2 * rpy:(y2 + 1) * rpy, tb:] = r_l[y2, rpy:2 * rpy, :]
        a1, a2, a3 = split3(rank_s[...])
        b1, b2, b3 = split3(scaled_s[...])
        low = dot_nn(a3, b1) + dot_nn(a2, b2) + dot_nn(a1, b3)
        u_s[...] = dot_nn(a1, b1) + (dot_nn(a2, b1) + dot_nn(a1, b2) + low)

        @pl.loop(0, ny)
        def _(y2):
            @pl.when(jnp.logical_not(jnp.logical_and(at_home, y2 == y)))
            def _():
                u_copy(y2).start()

        @pl.when(at_home)
        def _():
            gu[x, 2 * cl + y_par] = u_s[...]

        rows = up_g[xq, cl]
        low_s[...] = dot_tn(
            jnp.concatenate([a1, a2, a3], axis=0), jnp.concatenate([rows, rows, rows], axis=0)
        )

    def ux_copy(flow, step, h):
        slot = gu.at[wrap(x - sign_of(flow) * step, nx), pl.ds(h * (ny // 2), ny // 2)]
        return send_to(slot, slot, ux_ss, ux_rs.at[at(nx, 2, flow, step, h)], on_x(sign_of(flow)))

    def ux_arrival(flow, step, h):
        slot = gu.at[wrap(x - sign_of(flow) * (step + 1), nx), pl.ds(h * (ny // 2), ny // 2)]
        return send_to(slot, slot, ux_ss, ux_rs.at[at(nx, 2, flow, step, h)], on_x(sign_of(flow)))

    def dx_copy(flow, step, h):
        slot = gd.at[wrap(x - sign_of(flow) * step, nx), pl.ds(h * (ny // 2), ny // 2)]
        return send_to(slot, slot, dx_ss, dx_rs.at[at(nx, 2, flow, step, h)], on_x(sign_of(flow)))

    def dx_arrival(flow, step, h):
        slot = gd.at[wrap(x - sign_of(flow) * (step + 1), nx), pl.ds(h * (ny // 2), ny // 2)]
        return send_to(slot, slot, dx_ss, dx_rs.at[at(nx, 2, flow, step, h)], on_x(sign_of(flow)))

    def start_x(copy):
        for n in (0, 1):
            for flow in (0, 1):
                order = send_order(flow, 0, nx, 2)
                if n < len(order):
                    copy(flow, 0, order[n]).start()

    def pass_x(copy, arrival, step):
        if step >= nx // 2:
            return
        for n in (0, 1):
            for flow in (0, 1):
                order = send_order(flow, step, nx, 2)
                if n < len(order):
                    arrival(flow, step, order[n]).wait_recv()
                    if step + 1 < nx // 2 and order[n] in halves(flow, step + 1, nx, 2):
                        copy(flow, step + 1, order[n]).start()

    def after_u():
        by_home(lambda count: u_all(count).wait_recv(), ny)
        start_x(ux_copy)

    def dy_copy(i):
        slot = gd.at[x, y]
        return send_to(slot, slot, dy_ss, dy_rs, on_y(i))

    def dy_all():
        slots = gd.at[x, pl.ds(0, ny - 1)]
        return send_to(slots, slots, dy_ss, dy_rs, on_y(1))

    def after_h():
        h_all().wait_recv()

        for c in range(s_per):
            tile = h_l[c]
            for xb in range(1, nx):
                tile = tile + h_l[xb * s_per + c]
            tile = jnp.concatenate([tile, jnp.zeros((8 - 2 * rpy, tb), F32)], axis=0) if rpy < 4 else tile
            stacked = jnp.concatenate([v.astype(F32) for v in split3(tile)] + [jnp.zeros_like(tile)], axis=0)
            stacked = stacked.astype(BF16)
            both = []
            for p in (0, 1):
                full = dot_nn(stacked, tok_g[2 * c + p])
                both.append(full[0:8] + (full[8:16] + full[16:24]))
            gd[x, y, c * rpy:(c + 1) * rpy, :] = both[0][0:rpy] + both[1][rpy:2 * rpy]

        @pl.loop(1, ny)
        def _(i):
            dy_copy(i).start()

    def after_dy():
        dy_all().wait_recv()

        start_x(dx_copy)

    product(2 * place_of(0) + 1 - core)
    for n in (2, 3):
        for flow in (0, 1):
            first_copy(ring_order[flow][n]).start()
    product(2 * place_of(0) + core)
    send_rk()
    products(1, min(3, nz))
    ring_start()
    plan = []
    if half > 1:
        plan += [(0.1, lambda: ring_step(1, 0)), (0.2, lambda: ring_step(1, 1))]
        plan += [(3.3, lambda: ring_step(1, 2)), (4.6, lambda: ring_step(1, 3))]
    for step in range(2, half):
        for n in range(4):
            plan.append((5.9 + 5.2 * (step - 2) + 1.3 * n, functools.partial(ring_step, step, n)))
    plan += [
        (0.3, lambda: products(min(3, nz), min(5, nz))),
        (4.7, lambda: products(min(5, nz), nz)),
        (1.5, after_ex),
        (2.5, after_rk),
        (4.0, after_f),
        (5.0, after_r),
        (7.5, after_h),
        (9.5, after_u),
        (12.0, after_dy),
        (13.5, lambda: pass_x(ux_copy, ux_arrival, 0)),
        (16.0, lambda: pass_x(dx_copy, dx_arrival, 0)),
        (17.0, lambda: pass_x(ux_copy, ux_arrival, 1)),
    ]
    plan.sort(key=lambda item: item[0])
    for _, action in plan:
        action()
    gu_write = pltpu.make_async_copy(gu, gu_out, out_s.at[0])
    gu_write.start()

    norm, scaling = norms["norm"], norms["scaling"]

    def pr_copy(p, j):
        return send_to(proj_s.at[p, j], proj_l.at[y_par, j], pr_ss.at[p], pr_rs.at[y_par], on_swap(p))

    def pr_all(p):
        return send_to(proj_l.at[p], proj_l.at[p], pr_ss.at[p], pr_rs.at[p], on_swap(p))

    def send_pr(p, j):
        @pl.when(jnp.logical_not(stays[p]))
        def _():
            pr_copy(p, j).start()

        @pl.when(stays[p])
        def _():
            proj_l[p, j] = proj_s[p, j]

    sib_arrival(nz - 1).wait_recv()
    for q in range(4):
        p, j = q // 2, q % 2
        parts[t, q] = parts[t, q] + sib[z, q] + low_s[p * tb:(p + 1) * tb, j * hb:(j + 1) * hb]
    mag_sum = [None, None]
    for n in range(4):
        for flow in (0, 1):
            q = order_at(flow, half - 1)[n]
            if ring_has(flow, half - 1, q):
                ring_copy(flow, half - 1, q).wait_recv()
        for q in ([n] if half > 2 else [0, 2] if n == 2 else [1, 3] if n == 3 else []):
            p, j = q // 2, q % 2
            lanes = slice(j * hb, (j + 1) * hb)
            value = parts[t, q]
            for flow in (0, 1):
                if ring_has(flow, half - 1, q):
                    value = value + ring[flow, half - 1, q]
            proj_s[p, j] = (value * scaling[:, lanes]).astype(BF16)

            if n < 3:
                send_pr(p, j)
            term = jnp.sum(cot_l[p, :, lanes].astype(F32) * value, axis=0, keepdims=True)
            mag_sum[j] = term if mag_sum[j] is None else mag_sum[j] + term

    for j in (0, 1):
        m_s[j:j + 1, :] = mag_sum[j] / norm[:, j * hb:(j + 1) * hb]

    own_m = (x * s_per + cl) * 2 + y_par

    def m_copy(i):
        return send_to(m_s, m_g.at[own_m], m_ss, m_rs, target(i))

    def m_all(count):
        slots = m_g.at[pl.ds(0, count)]
        return send_to(slots, slots, m_ss, m_rs, on_x(1))

    for i in range(1, outs):
        m_copy(i).start()

    @pl.when(away)
    def _():
        m_copy(0).start()

    @pl.when(at_home)
    def _():
        m_g[own_m] = m_s[...]

    for q in (3,) if half > 2 else (1, 3):
        send_pr(q // 2, q % 2)

    def proj_write(p, j):
        return pltpu.make_async_copy(
            proj_l.at[p, j], proj_out.at[:, pl.ds(p * cb + j * hb, hb)], out_s.at[2 + 2 * p + j]
        )

    for p in (0, 1):
        @pl.when(jnp.logical_not(stays[p]))
        def _():
            pr_all(p).wait_recv()
            pr_all(p).wait_send()

        for j in (0, 1):
            proj_write(p, j).start()


    pass_x(dx_copy, dx_arrival, 1)
    gd_write = pltpu.make_async_copy(gd, gd_out, out_s.at[1])
    gd_write.start()

    def left(ref, send_sem, recv_sem):
        send_to(ref, ref, send_sem, recv_sem, on_y(1)).wait_send()

    left(tok_g.at[pl.ds(0, ny - 1)], tok_ss, tok_rs.at[0])
    left(w_g.at[pl.ds(0, nx - 1)], w_ss, w_rs.at[0])
    left(gu.at[pl.ds(0, nx - 1)], ux_ss, ux_rs.at[0])
    left(parts.at[pl.ds(0, nz - 1)], ring_ss, ring_rs.at[0])
    left(parts.at[pl.ds(0, nz)], sib_ss, sib_rs.at[0])
    up_all().wait_send()
    ex_all().wait_send()
    rk_all().wait_send()
    f_all().wait_send()
    r_all().wait_send()
    h_all().wait_send()
    dy_all().wait_send()
    by_home(lambda count: u_all(count).wait_send(), ny)
    for p in (0, 1):
        @pl.when(jnp.logical_not(stays[p]))
        def _():
            cot_copy(p).wait_send()
            mag_copy(p).wait_send()

    by_home(lambda count: m_all(count).wait_recv(), outs)
    by_home(lambda count: m_all(count).wait_send(), outs)
    left(gd.at[pl.ds(0, nx - 1)], dx_ss, dx_rs.at[0])
    m_write = pltpu.make_async_copy(m_g, m_out, out_s.at[6])
    m_write.start()
    gu_write.wait()
    gd_write.wait()
    for p in (0, 1):
        for j in (0, 1):
            proj_write(p, j).wait()
    m_write.wait()


def scatter_kernel(
    nx, ny, tenant_in, proj_in, gu_in, gd_in, m_in, proj_out, down_out, up_out, mag_out,
    tenant, proj, gu, gd, m, down, up, mag, sems,
):
    s_per = ny // 2
    rpy = RANK // ny
    hb = m.shape[2]
    cb = 2 * hb
    ins = ((tenant_in, tenant), (gu_in, gu), (gd_in, gd), (m_in, m), (proj_in, proj))
    outs = ((up, up_out), (down, down_out), (mag, mag_out), (proj, proj_out))
    reads = [pltpu.make_async_copy(src, dst, sems.at[n]) for n, (src, dst) in enumerate(ins)]
    writes = [pltpu.make_async_copy(src, dst, sems.at[5 + n]) for n, (src, dst) in enumerate(outs)]
    for read in reads:
        read.start()
    up[...] = jnp.zeros_like(up)
    down[...] = jnp.zeros_like(down)
    reads[0].wait()
    who = [tenant[n] for n in range(nx * s_per)]
    reads[1].wait()
    for n in range(nx * s_per):
        for p in (0, 1):
            up[who[n], :, cb * p:cb * (p + 1)] += gu[n // s_per, 2 * (n % s_per) + p]
    writes[0].start()
    reads[2].wait()
    for n in range(nx * s_per):
        c = n % s_per
        rows = [gd[n // s_per, yb, c * rpy:(c + 1) * rpy, :] for yb in range(ny)]
        down[who[n]] += jnp.concatenate(rows, axis=0)
    writes[1].start()
    reads[4].wait()
    writes[3].start()
    reads[3].wait()
    row_ids = lax.broadcasted_iota(jnp.int32, (mag.shape[0], hb), 0)
    sums = [jnp.zeros(row_ids.shape, F32)] * 4
    for n in range(nx * s_per):
        for q in range(4):
            sums[q] = sums[q] + jnp.where(row_ids == who[n], m[2 * n + q // 2, q % 2:q % 2 + 1, :], 0.0)
    for q in range(4):
        mag[:, hb * q:hb * (q + 1)] = sums[q]
    writes[2].start()
    for write in writes:
        write.wait()


def per_device(nx, ny, nt, tokens, base_weight, adapter_down, adapter_up, magnitude, tenant, cotangent):
    tb, kb = tokens.shape
    cb = base_weight.shape[1]
    hb = cb // 2
    tenants = adapter_down.shape[0]
    s_per = ny // 2
    nz = nt // 2
    rpy = RANK // ny
    dma = pltpu.SemaphoreType.DMA
    vmem = pl.BlockSpec(memory_space=pltpu.VMEM)
    hbm = pl.BlockSpec(memory_space=pltpu.HBM)
    scratch = [
        pltpu.SMEM(tenant.shape, jnp.int32),
        pltpu.VMEM(adapter_down.shape, BF16),
        pltpu.VMEM(adapter_up.shape, BF16),
        pltpu.VMEM(magnitude.shape, F32),
        pltpu.VMEM(cotangent.shape, BF16),
        pltpu.VMEM((ny, tb, kb), BF16),
        pltpu.VMEM((nx, kb, cb), BF16),
        pltpu.VMEM((nx, s_per, RANK, cb), BF16),
        pltpu.VMEM((nx, s_per, RANK, cb), BF16),
        pltpu.VMEM((s_per, RANK, kb), BF16),
        pltpu.VMEM((2, tb, cb), BF16),
        pltpu.VMEM((2, 8, cb), F32),
        pltpu.VMEM((2, 8, cb), F32),
        pltpu.VMEM((nt, 2, hb), F32),
        pltpu.VMEM((nt, 2, hb), F32),
        pltpu.VMEM((s_per, 2 * rpy, tb), F32),
        pltpu.VMEM((nt, 2 * rpy, tb), F32),
        pltpu.VMEM((ny, RANK, tb), F32),
        pltpu.VMEM((nt, 4, tb, hb), F32),
        pltpu.VMEM((nz, 4, tb, hb), F32),
        pltpu.VMEM((2, nz // 2, 4, tb, hb), F32),
        pltpu.VMEM((2 * tb, cb), F32),
        pltpu.VMEM((ny, 2 * rpy, tb), F32),
        pltpu.VMEM((ny, 2 * rpy, tb), F32),
        pltpu.VMEM((2 * rpy, tb), F32),
        pltpu.VMEM((ny, 2 * rpy, tb), F32),
        pltpu.VMEM((2 * rpy, tb), F32),
        pltpu.VMEM((nt, 2 * rpy, tb), F32),
        pltpu.VMEM((RANK, 2 * tb), F32),
        pltpu.VMEM((RANK, cb), F32),
        pltpu.VMEM((nx, ny, RANK, cb), F32),
        pltpu.VMEM((nx, ny, s_per * rpy, kb), F32),
        pltpu.VMEM((2 * tb, cb), F32),
        pltpu.VMEM((2, 2, tb, hb), BF16),
        pltpu.VMEM((2, 2, tb, hb), BF16),
        pltpu.VMEM((2, hb), F32),
        pltpu.VMEM((nx * ny, 2, hb), F32),
        dma((7,)),
    ]
    tok_n, w_n, x_n, ring_n = 4 * (ny - 1), 4 * (nx - 1), 2 * (nx - 1), 4 * (nz - 1)
    pairs = [
        (1, tok_n), (1, w_n), (1, 1), (2, 2), (2, 2), (1, 1), (1, 1), (1, nz), (1, ring_n),
        (1, 1), (1, 1), (1, 1), (1, 1), (1, x_n), (1, 1), (1, x_n), (2, 2), (1, 1),
    ]
    for place, pair in enumerate(pairs):
        scratch += [dma if count == 1 else dma((count,)) for count in pair]
        if place == 7:
            scratch.append(dma((4,)))
    scratch.append(dma((7,)))
    proj, up_terms, down_terms, mags = pl.pallas_call(
        functools.partial(exchange_kernel, nx, ny, nt),
        out_shape=(
            jax.ShapeDtypeStruct((tb, 2 * cb), BF16),
            jax.ShapeDtypeStruct((nx, ny, RANK, cb), F32),
            jax.ShapeDtypeStruct((nx, ny, s_per * rpy, kb), F32),
            jax.ShapeDtypeStruct((nx * ny, 2, hb), F32),
        ),
        in_specs=[hbm] * 7,
        out_specs=(hbm,) * 4,
        scratch_shapes=scratch,
        compiler_params=pltpu.CompilerParams(
            collective_id=0, has_side_effects=True, vmem_limit_bytes=60 * 1024 * 1024
        ),
        name="exchange",
    )(tenant, tokens, base_weight, adapter_down, adapter_up, magnitude, cotangent)
    return pl.pallas_call(
        functools.partial(scatter_kernel, nx, ny),
        out_shape=(
            jax.ShapeDtypeStruct((tb, 2 * cb), BF16),
            jax.ShapeDtypeStruct((tenants, RANK, kb), F32),
            jax.ShapeDtypeStruct((tenants, RANK, 2 * cb), F32),
            jax.ShapeDtypeStruct((tenants, 2 * cb), F32),
        ),
        in_specs=[hbm] * 5,
        out_specs=(hbm,) * 4,
        scratch_shapes=[
            pltpu.SMEM(tenant.shape, jnp.int32),
            pltpu.VMEM(proj.shape, BF16),
            pltpu.VMEM(up_terms.shape, F32),
            pltpu.VMEM(down_terms.shape, F32),
            pltpu.VMEM(mags.shape, F32),
            pltpu.VMEM((tenants, RANK, kb), F32),
            pltpu.VMEM((tenants, RANK, 2 * cb), F32),
            pltpu.VMEM((tenants, 2 * cb), F32),
            dma((9,)),
        ],
        compiler_params=pltpu.CompilerParams(vmem_limit_bytes=60 * 1024 * 1024),
        name="scatter",
    )(tenant, proj, up_terms, down_terms, mags)


def solution(mesh, nx=X_CHIPS):
    ny = mesh.shape["dp"] // nx
    nt = mesh.shape["tensor"]
    in_specs = (
        P("dp", "tensor"),
        P("tensor", "dp"),
        P(None, None, "tensor"),
        P(None, None, "dp"),
        P(None, "tensor"),
        P(),
        P("dp", "tensor"),
    )
    out_specs = (
        P("dp", "tensor"),
        P(None, None, "tensor"),
        P(None, None, "tensor"),
        P(None, "tensor"),
    )
    return jax.shard_map(
        functools.partial(per_device, nx, ny, nt),
        mesh=mesh, in_specs=in_specs, out_specs=out_specs, check_vma=False,
    )
```

```python
import functools

import jax
import jax.numpy as jnp
from jax import lax
from jax.experimental import pallas as pl
from jax.experimental.pallas import tpu as pltpu
from jax.sharding import PartitionSpec as P

X_CHIPS = 4
RANK = 16
F32 = jnp.float32
BF16 = jnp.bfloat16


def send_to(src, dst, send_sem, recv_sem, device):
    return pltpu.make_async_remote_copy(
        src_ref=src,
        dst_ref=dst,
        send_sem=send_sem,
        recv_sem=recv_sem,
        device_id=device,
        device_id_type=pl.DeviceIdType.MESH,
    )


def split3(value):
    high = value.astype(BF16)
    rest = value - high.astype(F32)
    middle = rest.astype(BF16)
    low = (rest - middle.astype(F32)).astype(BF16)
    return high, middle, low


def dot_nn(a, b):
    return jnp.dot(a, b, preferred_element_type=F32)


def dot_nt(a, b):
    return lax.dot_general(a, b, (((1,), (1,)), ((), ())), preferred_element_type=F32)


def dot_tn(a, b):
    return lax.dot_general(a, b, (((0,), (0,)), ((), ())), preferred_element_type=F32)


def halves(flow, step, count, pieces):
    if step < count // 2 - 1:
        return tuple(range(pieces))
    return tuple(range(pieces // 2)) if flow == 0 else tuple(range(pieces // 2, pieces))


def send_order(flow, step, count, pieces):
    chosen = halves(flow, step, count, pieces)
    if flow == 1 and len(chosen) == pieces:
        chosen = chosen[pieces // 2:] + chosen[:pieces // 2]
    return chosen


def exchange_kernel(
    nx, ny, nt,
    tenant_in, tok, w, down, up, mag, cot,
    proj_out, gu_out, gd_out, m_out,
    tenant, down_v, up_v, mag_v, cot_v, tok_g, w_g, up_sel, up_g, down_sel, cot_l, mag_s, mag_l,
    ex_s, ex_l, rk_s, rk_l, rank_p, parts, sib, ring,
    scaled_s, f_s, f_l, h_s, h_l, rank_s, u_s, gu, gd, low_s, proj_s, proj_l, m_s, m_g,
    in_s, tok_ss, tok_rs, w_ss, w_rs, up_ss, up_rs, cot_ss, cot_rs, mag_ss, mag_rs,
    ex_ss, ex_rs, rk_ss, rk_rs, sib_ss, sib_rs, first_rs, ring_ss, ring_rs, f_ss, f_rs, h_ss, h_rs,
    u_ss, u_rs, ux_ss, ux_rs, dy_ss, dy_rs, dx_ss, dx_rs, pr_ss, pr_rs, m_ss, m_rs, out_s,
):
    s_per = ny // 2
    nz = nt // 2
    half = nz // 2
    rpy = RANK // ny
    tb, kb = tok.shape
    cb = w.shape[1]
    hb = cb // 2
    dp = lax.axis_index("dp")
    t = lax.axis_index("tensor")
    x, y = lax.div(dp, ny), lax.rem(dp, ny)
    z, core = lax.div(t, 2), lax.rem(t, 2)
    xq, cl = lax.div(t, s_per), lax.rem(t, s_per)
    y_half, y_par = lax.div(y, 2), lax.rem(y, 2)
    at_home = y_half == cl
    away = jnp.logical_not(at_home)
    t_out = s_per * xq + y_half

    def dev(x2, y2, t2):
        return (x2 * ny + y2, t2)

    def wrap(value, count):
        return lax.rem(value + 2 * count, count)

    def on_y(i):
        return dev(x, wrap(y + i, ny), t)

    def on_x(i):
        return dev(wrap(x + i, nx), y, t)

    def on_t(i):
        return dev(x, y, wrap(t + i, nt))

    def on_z(i):
        return dev(x, y, 2 * wrap(z + i, nz) + core)

    def on_swap(p):
        return dev(x, 2 * cl + p, t_out)

    sibling = dev(x, y, 2 * z + 1 - core)
    stays = [jnp.logical_and(at_home, y_par == p) for p in (0, 1)]

    fetches = [
        pltpu.make_async_copy(src, dst, in_s.at[n])
        for n, (src, dst) in enumerate((
            (w, w_g.at[x]), (up, up_v), (down, down_v), (mag, mag_v), (tok, tok_g.at[y]), (cot, cot_v),
            (tenant_in, tenant),
        ))
    ]
    for fetch in fetches:
        fetch.start()
    barrier = pltpu.get_barrier_semaphore()

    def greet(device):
        pl.semaphore_signal(barrier, inc=1, device_id=device, device_id_type=pl.DeviceIdType.MESH)

    @pl.loop(1, ny)
    def _(i):
        greet(on_y(i))

    @pl.loop(1, nx)
    def _(i):
        greet(on_x(i))

    @pl.loop(1, nt)
    def _(i):
        greet(on_t(i))

    outs = nx * ny

    def target(i):
        return (wrap(dp + i, outs), t_out)

    for xb in range(nx):
        for c in range(s_per):
            for p in (0, 1):
                maker = dev(xb, 2 * cl + p, s_per * xq + c)

                @pl.when(jnp.logical_not(jnp.logical_and(maker[0] == dp, maker[1] == t)))
                def _():
                    greet(maker)

    others = (ny - 1) + (nx - 1) + (nt - 1)

    @pl.when(at_home)
    def _():
        pl.semaphore_wait(barrier, others + outs - 1)

    @pl.when(away)
    def _():
        pl.semaphore_wait(barrier, others + outs)

    pieces = 4
    tp, wp = tb // pieces, kb // pieces

    def sign_of(flow):
        return 1 if flow == 0 else -1

    def at(count, many, flow, step, h):
        before = sum(len(halves(flow, k, count, many)) for k in range(step))
        place = halves(flow, step, count, many).index(h)
        return flow * (count - 1) * many // 2 + before + place

    def tok_copy(flow, step, h):
        sign = sign_of(flow)
        slot = tok_g.at[wrap(y - sign * step, ny), pl.ds(h * tp, tp)]
        src = tok.at[pl.ds(h * tp, tp)] if step == 0 else slot
        return send_to(src, slot, tok_ss, tok_rs.at[at(ny, pieces, flow, step, h)], on_y(sign))

    def tok_arrival(flow, step, h):
        sign = sign_of(flow)
        slot = tok_g.at[wrap(y - sign * (step + 1), ny), pl.ds(h * tp, tp)]
        return send_to(slot, slot, tok_ss, tok_rs.at[at(ny, pieces, flow, step, h)], on_y(sign))

    def w_copy(flow, step, h):
        sign = sign_of(flow)
        slot = w_g.at[wrap(x - sign * step, nx), pl.ds(h * wp, wp)]
        src = w.at[pl.ds(h * wp, wp)] if step == 0 else slot
        return send_to(src, slot, w_ss, w_rs.at[at(nx, pieces, flow, step, h)], on_x(sign))

    def w_arrival(flow, step, h):
        sign = sign_of(flow)
        slot = w_g.at[wrap(x - sign * (step + 1), nx), pl.ds(h * wp, wp)]
        return send_to(slot, slot, w_ss, w_rs.at[at(nx, pieces, flow, step, h)], on_x(sign))

    def up_copy(i):
        return send_to(up_sel.at[wrap(x + i, nx)], up_g.at[x], up_ss, up_rs, on_x(i))

    def up_all():
        slots = up_g.at[pl.ds(0, nx - 1)]
        return send_to(slots, slots, up_ss, up_rs, on_x(1))

    for flow in (0, 1):
        tok_copy(flow, 0, send_order(flow, 0, ny, pieces)[0]).start()
        w_copy(flow, 0, send_order(flow, 0, nx, pieces)[0]).start()

    for n in (6, 1, 2, 3):
        fetches[n].wait()
    for c in range(nx * s_per):
        up_sel[c // s_per, c % s_per] = up_v[tenant[c]]
    up_g[x] = up_sel[x]
    for c in range(s_per):
        down_sel[c] = down_v[tenant[x * s_per + c]]
    row_ids = lax.broadcasted_iota(jnp.int32, mag_v.shape, 0)
    mag_row = jnp.sum(jnp.where(row_ids == tenant[x * s_per + y_half], mag_v[...], 0.0), axis=0, keepdims=True)
    for p in (0, 1):
        mag_s[p] = jnp.broadcast_to(mag_row[:, p * cb:(p + 1) * cb], (8, cb))

    for i in range(1, nx):
        up_copy(i).start()

    for place in range(1, pieces):
        for flow in (0, 1):
            order = send_order(flow, 0, ny, pieces)
            if place < len(order):
                tok_copy(flow, 0, order[place]).start()
            order = send_order(flow, 0, nx, pieces)
            if place < len(order):
                w_copy(flow, 0, order[place]).start()

    def cot_copy(p):
        return send_to(cot_v.at[:, pl.ds(p * cb, cb)], cot_l.at[y_par], cot_ss.at[p], cot_rs.at[y_par], on_swap(p))

    def cot_arrival(p):
        return send_to(cot_l.at[p], cot_l.at[p], cot_ss.at[p], cot_rs.at[p], on_swap(p))

    def mag_copy(p):
        return send_to(mag_s.at[p], mag_l.at[y_par], mag_ss.at[p], mag_rs.at[y_par], on_swap(p))

    def mag_arrival(p):
        return send_to(mag_l.at[p], mag_l.at[p], mag_ss.at[p], mag_rs.at[p], on_swap(p))

    def send_cot():
        fetches[5].wait()
        for p in (0, 1):
            @pl.when(jnp.logical_not(stays[p]))
            def _():
                cot_copy(p).start()
                mag_copy(p).start()

            @pl.when(stays[p])
            def _():
                cot_l[p] = cot_v[:, p * cb:(p + 1) * cb]
                mag_l[p] = mag_s[p]

    def rank_of(block):
        rank_p[block] = dot_nt(down_sel[lax.div(block, 2)], tok_g[block])

    def squares_of(xb):
        block = w_g[xb]
        block_f32 = block.astype(F32)
        base = jnp.sum(block_f32 * block_f32, axis=0, keepdims=True)
        crossed = dot_nn(down_sel[...].reshape(s_per * RANK, kb), block)
        for c in range(s_per):
            rows = up_g[xb, c]
            quad = dot_tn(grams[c], jnp.concatenate([rows, rows, rows], axis=0))
            mixed = rows.astype(F32) * (2.0 * crossed[c * RANK:(c + 1) * RANK] + quad)
            squares = base + jnp.sum(mixed, axis=0, keepdims=True)
            ex_s[xb * s_per + c, 0:1, :] = squares[:, :hb]
            ex_s[xb * s_per + c, 1:2, :] = squares[:, hb:]

    def ex_copy(i):
        return send_to(ex_s.at[wrap(t + i, nt)], ex_l.at[t], ex_ss, ex_rs, on_t(i))

    def ex_all():
        slots = ex_l.at[pl.ds(0, nt - 1)]
        return send_to(slots, slots, ex_ss, ex_rs, on_t(1))

    def rk_copy(i):
        return send_to(rk_s.at[lax.rem(wrap(t + i, nt), s_per)], rk_l.at[t], rk_ss, rk_rs, on_t(i))

    def rk_all():
        slots = rk_l.at[pl.ds(0, nt - 1)]
        return send_to(slots, slots, rk_ss, rk_rs, on_t(1))

    def send_ex():
        @pl.loop(1, nt)
        def _(i):
            ex_copy(i).start()

        ex_l[t] = ex_s[t]

    def send_rk():
        for c in range(s_per):
            for p in (0, 1):
                own = rank_p[2 * c + p]
                picked = own[0:rpy]
                for y2 in range(1, ny):
                    picked = jnp.where(y == y2, own[y2 * rpy:(y2 + 1) * rpy], picked)
                rk_s[c, p * rpy:(p + 1) * rpy, :] = picked

        @pl.loop(1, nt)
        def _(i):
            rk_copy(i).start()

        rk_l[t] = rk_s[cl]

    grams = []
    for c in range(s_per):
        rows = down_sel[c]
        grams.append(jnp.concatenate(split3(dot_nt(rows, rows)), axis=0))
    fetches[0].wait()
    squares_of(x)
    fetches[4].wait()
    rank_of(y)

    events = []
    for flow in (0, 1):
        for step in range(ny // 2):
            for n, h in enumerate(send_order(flow, step, ny, pieces)):
                events.append((2.65 + 2.65 * step + 0.65 * n, 0, flow, step, h))
        for step in range(nx // 2):
            for n, h in enumerate(send_order(flow, step, nx, pieces)):
                events.append((3.3 + 5.2 * step + 1.3 * n, 1, flow, step, h))
    events.sort()
    last = {}
    for n, (_, kind, flow, step, h) in enumerate(events):
        last[kind, step] = n
    cot_at = last[0, max(ny // 2 - 2, 0)]
    for n, (_, kind, flow, step, h) in enumerate(events):
        arrival, copy, count = (tok_arrival, tok_copy, ny) if kind == 0 else (w_arrival, w_copy, nx)
        arrival(flow, step, h).wait_recv()
        if step + 1 < count // 2 and h in halves(flow, step + 1, count, pieces):
            copy(flow, step + 1, h).start()
        if n == cot_at:
            send_cot()
        if n == last[kind, step]:
            if kind == 0:
                rank_of(wrap(y + step + 1, ny))
                if step + 1 < ny // 2:
                    rank_of(wrap(y - step - 1, ny))
            else:
                if step == 0:
                    up_all().wait_recv()
                squares_of(wrap(x + step + 1, nx))
                if step + 1 < nx // 2:
                    squares_of(wrap(x - step - 1, nx))
                if step + 1 == nx // 2:
                    send_ex()

    def stretch_tokens(c):
        return tok_g[pl.ds(2 * c, 2)].reshape(2 * tb, kb)

    def place_of(i):
        return wrap(z + half + (1 - 2 * lax.rem(i, 2)) * lax.div(i + 1, 2), nz)

    def product(slot):
        xb, c = lax.div(slot, s_per), lax.rem(slot, s_per)
        result = dot_nn(stretch_tokens(c), w_g[xb])
        for p in (0, 1):
            for j in (0, 1):
                parts[slot, 2 * p + j] = result[p * tb:(p + 1) * tb, j * hb:(j + 1) * hb]

    def sib_copy(i):
        zb = place_of(i)
        return send_to(parts.at[2 * zb + 1 - core], sib.at[zb], sib_ss, sib_rs.at[i], sibling)

    def sib_arrival(i):
        slot = sib.at[place_of(i)]
        return send_to(slot, slot, sib_ss, sib_rs.at[i], sibling)

    def first_copy(q):
        zb = place_of(0)
        return send_to(parts.at[2 * zb + 1 - core, q], sib.at[zb, q], sib_ss, first_rs.at[q], sibling)

    def products(first, end):
        @pl.loop(first, end)
        def _(i):
            product(2 * place_of(i) + 1 - core)
            sib_copy(i).start()
            product(2 * place_of(i) + core)

    def ring_at(flow, step, q):
        return flow * (nz - 1) * 2 + (q % 2 if step == 0 else 2 + 4 * (step - 1) + q)

    def ring_copy(flow, step, q):
        sign = sign_of(flow)
        zb = wrap(z + sign * (half - step), nz)
        return send_to(
            parts.at[2 * zb + core, q], ring.at[flow, step, q],
            ring_ss, ring_rs.at[ring_at(flow, step, q)], on_z(sign),
        )

    def ring_has(flow, step, q):
        return step > 0 or q // 2 == flow

    def ring_send(flow, step, q):
        zb = wrap(z + sign_of(flow) * (half - step), nz)
        value = parts[2 * zb + core, q] + sib[zb, q]
        if step > 0 and ring_has(flow, step - 1, q):
            ring_copy(flow, step - 1, q).wait_recv()
            value = value + ring[flow, step - 1, q]
        parts[2 * zb + core, q] = value
        ring_copy(flow, step, q).start()

    ring_order = ((2, 3, 0, 1), (0, 1, 2, 3))

    def order_at(flow, step):
        return ring_order[flow] if step < 2 else (0, 1, 2, 3)


    def ring_start():
        for n in (2, 3):
            for flow in (0, 1):
                q = ring_order[flow][n]
                first_copy(q).wait_recv()
                ring_send(flow, 0, q)

    def ring_step(step, n):
        if n == 0:
            sib_arrival(2 * step - 1).wait_recv()
            sib_arrival(2 * step).wait_recv()
        for flow in (0, 1):
            ring_send(flow, step, order_at(flow, step)[n])

    norms = {}

    def after_ex():
        ex_all().wait_recv()

        for p in (0, 1):
            @pl.when(jnp.logical_not(stays[p]))
            def _():
                cot_arrival(p).wait_recv()
                mag_arrival(p).wait_recv()

        total = jnp.sum(ex_l[...], axis=0)
        squares = jnp.concatenate([total[0:1], total[1:2]], axis=1)
        norm = jnp.sqrt(squares + 1e-06)
        scaling = mag_l[0][0:1] / norm
        scaled = cot_l[...].reshape(2 * tb, cb).astype(F32) * scaling
        scaled_s[...] = scaled
        rows = up_g[xq, cl]
        parts3 = split3(scaled)
        back = dot_nt(rows, parts3[0]) + (dot_nt(rows, parts3[1]) + dot_nt(rows, parts3[2]))
        rk_all().wait_recv()
        ranks = jnp.sum(rk_l[...], axis=0)
        for y2 in range(ny):
            f_s[y2, 2 * rpy:4 * rpy, :] = ranks
            f_s[y2, 0:rpy, :] = back[y2 * rpy:(y2 + 1) * rpy, :tb]
            f_s[y2, rpy:2 * rpy, :] = back[y2 * rpy:(y2 + 1) * rpy, tb:]

        @pl.loop(1, ny)
        def _(i):
            f_copy(i).start()

        f_l[y] = f_s[y]
        norms["norm"], norms["scaling"] = norm, scaling

    def f_copy(i):
        return send_to(f_s.at[wrap(y + i, ny)], f_l.at[y], f_ss, f_rs, on_y(i))

    def f_all():
        slots = f_l.at[pl.ds(0, ny - 1)]
        return send_to(slots, slots, f_ss, f_rs, on_y(1))

    def h_copy(i):
        return send_to(h_s, h_l.at[t], h_ss, h_rs, on_t(i))

    def h_all():
        slots = h_l.at[pl.ds(0, nt - 1)]
        return send_to(slots, slots, h_ss, h_rs, on_t(1))

    def after_f():
        f_all().wait_recv()

        h_s[...] = jnp.sum(f_l[:, 0:2 * rpy, :], axis=0)

        @pl.loop(1, nt)
        def _(i):
            h_copy(i).start()

        h_l[t] = h_s[...]

    def u_copy(y2):
        return send_to(u_s, gu.at[x, 2 * cl + y_par], u_ss, u_rs, dev(x, y2, t_out))

    def u_all(count):
        slots = gu.at[x, pl.ds(0, count)]
        return send_to(slots, slots, u_ss, u_rs, on_x(1))

    def by_home(wait, count):
        @pl.when(at_home)
        def _():
            wait(count - 1)

        @pl.when(away)
        def _():
            wait(count)

    def after_r():

        for y2 in range(ny):
            rank_s[y2 * rpy:(y2 + 1) * rpy, :tb] = f_l[y2, 2 * rpy:3 * rpy, :]
            rank_s[y2 * rpy:(y2 + 1) * rpy, tb:] = f_l[y2, 3 * rpy:4 * rpy, :]
        a1, a2, a3 = split3(rank_s[...])
        b1, b2, b3 = split3(scaled_s[...])
        low = dot_nn(a3, b1) + dot_nn(a2, b2) + dot_nn(a1, b3)
        u_s[...] = dot_nn(a1, b1) + (dot_nn(a2, b1) + dot_nn(a1, b2) + low)

        @pl.loop(0, ny)
        def _(y2):
            @pl.when(jnp.logical_not(jnp.logical_and(at_home, y2 == y)))
            def _():
                u_copy(y2).start()

        @pl.when(at_home)
        def _():
            gu[x, 2 * cl + y_par] = u_s[...]

        rows = up_g[xq, cl]
        low_s[...] = dot_tn(
            jnp.concatenate([a1, a2, a3], axis=0), jnp.concatenate([rows, rows, rows], axis=0)
        )

    def ux_copy(flow, step, h):
        slot = gu.at[wrap(x - sign_of(flow) * step, nx), pl.ds(h * (ny // 2), ny // 2)]
        return send_to(slot, slot, ux_ss, ux_rs.at[at(nx, 2, flow, step, h)], on_x(sign_of(flow)))

    def ux_arrival(flow, step, h):
        slot = gu.at[wrap(x - sign_of(flow) * (step + 1), nx), pl.ds(h * (ny // 2), ny // 2)]
        return send_to(slot, slot, ux_ss, ux_rs.at[at(nx, 2, flow, step, h)], on_x(sign_of(flow)))

    def dx_copy(flow, step, h):
        slot = gd.at[wrap(x - sign_of(flow) * step, nx), pl.ds(h * (ny // 2), ny // 2)]
        return send_to(slot, slot, dx_ss, dx_rs.at[at(nx, 2, flow, step, h)], on_x(sign_of(flow)))

    def dx_arrival(flow, step, h):
        slot = gd.at[wrap(x - sign_of(flow) * (step + 1), nx), pl.ds(h * (ny // 2), ny // 2)]
        return send_to(slot, slot, dx_ss, dx_rs.at[at(nx, 2, flow, step, h)], on_x(sign_of(flow)))

    def start_x(copy):
        for n in (0, 1):
            for flow in (0, 1):
                order = send_order(flow, 0, nx, 2)
                if n < len(order):
                    copy(flow, 0, order[n]).start()

    def pass_x(copy, arrival, step):
        if step >= nx // 2:
            return
        for n in (0, 1):
            for flow in (0, 1):
                order = send_order(flow, step, nx, 2)
                if n < len(order):
                    arrival(flow, step, order[n]).wait_recv()
                    if step + 1 < nx // 2 and order[n] in halves(flow, step + 1, nx, 2):
                        copy(flow, step + 1, order[n]).start()

    def after_u():
        by_home(lambda count: u_all(count).wait_recv(), ny)
        start_x(ux_copy)

    def dy_copy(i):
        slot = gd.at[x, y]
        return send_to(slot, slot, dy_ss, dy_rs, on_y(i))

    def dy_all():
        slots = gd.at[x, pl.ds(0, ny - 1)]
        return send_to(slots, slots, dy_ss, dy_rs, on_y(1))

    def after_h():
        h_all().wait_recv()

        for c in range(s_per):
            tile = h_l[c]
            for xb in range(1, nx):
                tile = tile + h_l[xb * s_per + c]
            tile = jnp.concatenate([tile, jnp.zeros((8 - 2 * rpy, tb), F32)], axis=0) if rpy < 4 else tile
            stacked = jnp.concatenate([v.astype(F32) for v in split3(tile)] + [jnp.zeros_like(tile)], axis=0)
            stacked = stacked.astype(BF16)
            both = []
            for p in (0, 1):
                full = dot_nn(stacked, tok_g[2 * c + p])
                both.append(full[0:8] + (full[8:16] + full[16:24]))
            gd[x, y, c * rpy:(c + 1) * rpy, :] = both[0][0:rpy] + both[1][rpy:2 * rpy]

        @pl.loop(1, ny)
        def _(i):
            dy_copy(i).start()

    def after_dy():
        dy_all().wait_recv()

        start_x(dx_copy)

    product(2 * place_of(0) + 1 - core)
    for n in (2, 3):
        for flow in (0, 1):
            first_copy(ring_order[flow][n]).start()
    product(2 * place_of(0) + core)
    send_rk()
    products(1, min(3, nz))
    ring_start()
    plan = []
    if half > 1:
        plan += [(0.1, lambda: ring_step(1, 0)), (0.2, lambda: ring_step(1, 1))]
        plan += [(3.3, lambda: ring_step(1, 2)), (4.6, lambda: ring_step(1, 3))]
    for step in range(2, half):
        for n in range(4):
            plan.append((5.9 + 5.2 * (step - 2) + 1.3 * n, functools.partial(ring_step, step, n)))
    plan += [
        (0.3, lambda: products(min(3, nz), min(5, nz))),
        (4.7, lambda: products(min(5, nz), nz)),
        (1.5, after_ex),
        (4.0, after_f),
        (5.0, after_r),
        (7.5, after_h),
        (9.5, after_u),
        (12.0, after_dy),
        (13.5, lambda: pass_x(ux_copy, ux_arrival, 0)),
        (16.0, lambda: pass_x(dx_copy, dx_arrival, 0)),
        (17.0, lambda: pass_x(ux_copy, ux_arrival, 1)),
    ]
    plan.sort(key=lambda item: item[0])
    for _, action in plan:
        action()
    gu_write = pltpu.make_async_copy(gu, gu_out, out_s.at[0])
    gu_write.start()

    norm, scaling = norms["norm"], norms["scaling"]

    def pr_copy(p, j):
        return send_to(proj_s.at[p, j], proj_l.at[y_par, j], pr_ss.at[p], pr_rs.at[y_par], on_swap(p))

    def pr_all(p):
        return send_to(proj_l.at[p], proj_l.at[p], pr_ss.at[p], pr_rs.at[p], on_swap(p))

    def send_pr(p, j):
        @pl.when(jnp.logical_not(stays[p]))
        def _():
            pr_copy(p, j).start()

        @pl.when(stays[p])
        def _():
            proj_l[p, j] = proj_s[p, j]

    sib_arrival(nz - 1).wait_recv()
    for q in range(4):
        p, j = q // 2, q % 2
        parts[t, q] = parts[t, q] + sib[z, q] + low_s[p * tb:(p + 1) * tb, j * hb:(j + 1) * hb]
    mag_sum = [None, None]
    for n in range(4):
        for flow in (0, 1):
            q = order_at(flow, half - 1)[n]
            if ring_has(flow, half - 1, q):
                ring_copy(flow, half - 1, q).wait_recv()
        for q in ([n] if half > 2 else [0, 2] if n == 2 else [1, 3] if n == 3 else []):
            p, j = q // 2, q % 2
            lanes = slice(j * hb, (j + 1) * hb)
            value = parts[t, q]
            for flow in (0, 1):
                if ring_has(flow, half - 1, q):
                    value = value + ring[flow, half - 1, q]
            proj_s[p, j] = (value * scaling[:, lanes]).astype(BF16)

            if n < 3:
                send_pr(p, j)
            term = jnp.sum(cot_l[p, :, lanes].astype(F32) * value, axis=0, keepdims=True)
            mag_sum[j] = term if mag_sum[j] is None else mag_sum[j] + term

    for j in (0, 1):
        m_s[j:j + 1, :] = mag_sum[j] / norm[:, j * hb:(j + 1) * hb]

    own_m = (x * s_per + cl) * 2 + y_par

    def m_copy(i):
        return send_to(m_s, m_g.at[own_m], m_ss, m_rs, target(i))

    def m_all(count):
        slots = m_g.at[pl.ds(0, count)]
        return send_to(slots, slots, m_ss, m_rs, on_x(1))

    for i in range(1, outs):
        m_copy(i).start()

    @pl.when(away)
    def _():
        m_copy(0).start()

    @pl.when(at_home)
    def _():
        m_g[own_m] = m_s[...]

    for q in (3,) if half > 2 else (1, 3):
        send_pr(q // 2, q % 2)

    def proj_write(p, j):
        return pltpu.make_async_copy(
            proj_l.at[p, j], proj_out.at[:, pl.ds(p * cb + j * hb, hb)], out_s.at[2 + 2 * p + j]
        )

    for p in (0, 1):
        @pl.when(jnp.logical_not(stays[p]))
        def _():
            pr_all(p).wait_recv()
            pr_all(p).wait_send()

        for j in (0, 1):
            proj_write(p, j).start()


    pass_x(dx_copy, dx_arrival, 1)
    gd_write = pltpu.make_async_copy(gd, gd_out, out_s.at[1])
    gd_write.start()

    def left(ref, send_sem, recv_sem):
        send_to(ref, ref, send_sem, recv_sem, on_y(1)).wait_send()

    left(tok_g.at[pl.ds(0, ny - 1)], tok_ss, tok_rs.at[0])
    left(w_g.at[pl.ds(0, nx - 1)], w_ss, w_rs.at[0])
    left(gu.at[pl.ds(0, nx - 1)], ux_ss, ux_rs.at[0])
    left(parts.at[pl.ds(0, nz - 1)], ring_ss, ring_rs.at[0])
    left(parts.at[pl.ds(0, nz)], sib_ss, sib_rs.at[0])
    up_all().wait_send()
    ex_all().wait_send()
    rk_all().wait_send()
    f_all().wait_send()
    h_all().wait_send()
    dy_all().wait_send()
    by_home(lambda count: u_all(count).wait_send(), ny)
    for p in (0, 1):
        @pl.when(jnp.logical_not(stays[p]))
        def _():
            cot_copy(p).wait_send()
            mag_copy(p).wait_send()

    by_home(lambda count: m_all(count).wait_recv(), outs)
    by_home(lambda count: m_all(count).wait_send(), outs)
    left(gd.at[pl.ds(0, nx - 1)], dx_ss, dx_rs.at[0])
    m_write = pltpu.make_async_copy(m_g, m_out, out_s.at[6])
    m_write.start()
    gu_write.wait()
    gd_write.wait()
    for p in (0, 1):
        for j in (0, 1):
            proj_write(p, j).wait()
    m_write.wait()


def scatter_kernel(
    nx, ny, tenant_in, proj_in, gu_in, gd_in, m_in, proj_out, down_out, up_out, mag_out,
    tenant, proj, gu, gd, m, down, up, mag, sems,
):
    s_per = ny // 2
    rpy = RANK // ny
    hb = m.shape[2]
    cb = 2 * hb
    ins = ((tenant_in, tenant), (gu_in, gu), (gd_in, gd), (m_in, m), (proj_in, proj))
    outs = ((up, up_out), (down, down_out), (mag, mag_out), (proj, proj_out))
    reads = [pltpu.make_async_copy(src, dst, sems.at[n]) for n, (src, dst) in enumerate(ins)]
    writes = [pltpu.make_async_copy(src, dst, sems.at[5 + n]) for n, (src, dst) in enumerate(outs)]
    for read in reads:
        read.start()
    up[...] = jnp.zeros_like(up)
    down[...] = jnp.zeros_like(down)
    reads[0].wait()
    who = [tenant[n] for n in range(nx * s_per)]
    reads[1].wait()
    for n in range(nx * s_per):
        for p in (0, 1):
            up[who[n], :, cb * p:cb * (p + 1)] += gu[n // s_per, 2 * (n % s_per) + p]
    writes[0].start()
    reads[2].wait()
    for n in range(nx * s_per):
        c = n % s_per
        rows = [gd[n // s_per, yb, c * rpy:(c + 1) * rpy, :] for yb in range(ny)]
        down[who[n]] += jnp.concatenate(rows, axis=0)
    writes[1].start()
    reads[4].wait()
    writes[3].start()
    reads[3].wait()
    row_ids = lax.broadcasted_iota(jnp.int32, (mag.shape[0], hb), 0)
    sums = [jnp.zeros(row_ids.shape, F32)] * 4
    for n in range(nx * s_per):
        for q in range(4):
            sums[q] = sums[q] + jnp.where(row_ids == who[n], m[2 * n + q // 2, q % 2:q % 2 + 1, :], 0.0)
    for q in range(4):
        mag[:, hb * q:hb * (q + 1)] = sums[q]
    writes[2].start()
    for write in writes:
        write.wait()


def per_device(nx, ny, nt, tokens, base_weight, adapter_down, adapter_up, magnitude, tenant, cotangent):
    tb, kb = tokens.shape
    cb = base_weight.shape[1]
    hb = cb // 2
    tenants = adapter_down.shape[0]
    s_per = ny // 2
    nz = nt // 2
    rpy = RANK // ny
    dma = pltpu.SemaphoreType.DMA
    vmem = pl.BlockSpec(memory_space=pltpu.VMEM)
    hbm = pl.BlockSpec(memory_space=pltpu.HBM)
    scratch = [
        pltpu.SMEM(tenant.shape, jnp.int32),
        pltpu.VMEM(adapter_down.shape, BF16),
        pltpu.VMEM(adapter_up.shape, BF16),
        pltpu.VMEM(magnitude.shape, F32),
        pltpu.VMEM(cotangent.shape, BF16),
        pltpu.VMEM((ny, tb, kb), BF16),
        pltpu.VMEM((nx, kb, cb), BF16),
        pltpu.VMEM((nx, s_per, RANK, cb), BF16),
        pltpu.VMEM((nx, s_per, RANK, cb), BF16),
        pltpu.VMEM((s_per, RANK, kb), BF16),
        pltpu.VMEM((2, tb, cb), BF16),
        pltpu.VMEM((2, 8, cb), F32),
        pltpu.VMEM((2, 8, cb), F32),
        pltpu.VMEM((nt, 2, hb), F32),
        pltpu.VMEM((nt, 2, hb), F32),
        pltpu.VMEM((s_per, 2 * rpy, tb), F32),
        pltpu.VMEM((nt, 2 * rpy, tb), F32),
        pltpu.VMEM((ny, RANK, tb), F32),
        pltpu.VMEM((nt, 4, tb, hb), F32),
        pltpu.VMEM((nz, 4, tb, hb), F32),
        pltpu.VMEM((2, nz // 2, 4, tb, hb), F32),
        pltpu.VMEM((2 * tb, cb), F32),
        pltpu.VMEM((ny, 4 * rpy, tb), F32),
        pltpu.VMEM((ny, 4 * rpy, tb), F32),
        pltpu.VMEM((2 * rpy, tb), F32),
        pltpu.VMEM((nt, 2 * rpy, tb), F32),
        pltpu.VMEM((RANK, 2 * tb), F32),
        pltpu.VMEM((RANK, cb), F32),
        pltpu.VMEM((nx, ny, RANK, cb), F32),
        pltpu.VMEM((nx, ny, s_per * rpy, kb), F32),
        pltpu.VMEM((2 * tb, cb), F32),
        pltpu.VMEM((2, 2, tb, hb), BF16),
        pltpu.VMEM((2, 2, tb, hb), BF16),
        pltpu.VMEM((2, hb), F32),
        pltpu.VMEM((nx * ny, 2, hb), F32),
        dma((7,)),
    ]
    tok_n, w_n, x_n, ring_n = 4 * (ny - 1), 4 * (nx - 1), 2 * (nx - 1), 4 * (nz - 1)
    pairs = [
        (1, tok_n), (1, w_n), (1, 1), (2, 2), (2, 2), (1, 1), (1, 1), (1, nz), (1, ring_n),
        (1, 1), (1, 1), (1, 1), (1, x_n), (1, 1), (1, x_n), (2, 2), (1, 1),
    ]
    for place, pair in enumerate(pairs):
        scratch += [dma if count == 1 else dma((count,)) for count in pair]
        if place == 7:
            scratch.append(dma((4,)))
    scratch.append(dma((7,)))
    proj, up_terms, down_terms, mags = pl.pallas_call(
        functools.partial(exchange_kernel, nx, ny, nt),
        out_shape=(
            jax.ShapeDtypeStruct((tb, 2 * cb), BF16),
            jax.ShapeDtypeStruct((nx, ny, RANK, cb), F32),
            jax.ShapeDtypeStruct((nx, ny, s_per * rpy, kb), F32),
            jax.ShapeDtypeStruct((nx * ny, 2, hb), F32),
        ),
        in_specs=[hbm] * 7,
        out_specs=(hbm,) * 4,
        scratch_shapes=scratch,
        compiler_params=pltpu.CompilerParams(
            collective_id=0, has_side_effects=True, vmem_limit_bytes=60 * 1024 * 1024
        ),
        name="exchange",
    )(tenant, tokens, base_weight, adapter_down, adapter_up, magnitude, cotangent)
    return pl.pallas_call(
        functools.partial(scatter_kernel, nx, ny),
        out_shape=(
            jax.ShapeDtypeStruct((tb, 2 * cb), BF16),
            jax.ShapeDtypeStruct((tenants, RANK, kb), F32),
            jax.ShapeDtypeStruct((tenants, RANK, 2 * cb), F32),
            jax.ShapeDtypeStruct((tenants, 2 * cb), F32),
        ),
        in_specs=[hbm] * 5,
        out_specs=(hbm,) * 4,
        scratch_shapes=[
            pltpu.SMEM(tenant.shape, jnp.int32),
            pltpu.VMEM(proj.shape, BF16),
            pltpu.VMEM(up_terms.shape, F32),
            pltpu.VMEM(down_terms.shape, F32),
            pltpu.VMEM(mags.shape, F32),
            pltpu.VMEM((tenants, RANK, kb), F32),
            pltpu.VMEM((tenants, RANK, 2 * cb), F32),
            pltpu.VMEM((tenants, 2 * cb), F32),
            dma((9,)),
        ],
        compiler_params=pltpu.CompilerParams(vmem_limit_bytes=60 * 1024 * 1024),
        name="scatter",
    )(tenant, proj, up_terms, down_terms, mags)


def solution(mesh, nx=X_CHIPS):
    ny = mesh.shape["dp"] // nx
    nt = mesh.shape["tensor"]
    in_specs = (
        P("dp", "tensor"),
        P("tensor", "dp"),
        P(None, None, "tensor"),
        P(None, None, "dp"),
        P(None, "tensor"),
        P(),
        P("dp", "tensor"),
    )
    out_specs = (
        P("dp", "tensor"),
        P(None, None, "tensor"),
        P(None, None, "tensor"),
        P(None, "tensor"),
    )
    return jax.shard_map(
        functools.partial(per_device, nx, ny, nt),
        mesh=mesh, in_specs=in_specs, out_specs=out_specs, check_vma=False,
    )
```
